32 devices in a mesh: cand: 4 (over z), slab: 8 (over y, x, core).
Axes of the slice: x: 2, y: 2, z: 4, core: 2. Of those that a mesh axis runs over, the one named last changes fastest.
Arguments:
- velocity: float32 [3, 32, 32, 128], P(None, 'slab'), may hold values from -6 to 6
- stress: float32 [6, 32, 32, 128], P(None, 'slab'), may hold values from -6 to 6
- lame_lambda: bfloat16 [32, 32, 128], P('slab'), may hold values from 0.5 to 1.5
- shear_modulus: bfloat16 [32, 32, 128], P('slab'), may hold values from 0.29882812 to 1
- buoyancy: bfloat16 [32, 32, 128], P('slab'), may hold values from 0.5 to 1.5
- surface: float32 [8, 6, 32, 32], P(None, None, 'slab', 'cand'), may hold values from -6 to 6
- block_owner: int32 [4], replicated, may hold values from 0 to 3, each once
- candidates: float32 [16, 3], replicated, may hold values from 0.7 to 1.4
- candidate_of_group: int32 [16], replicated, may hold values from 0 to 15, each once
Outputs:
- velocity_out: float32 [4, 3, 32, 32, 128], P('cand', None, 'slab')
- stress_out: float32 [4, 6, 32, 32, 128], P('cand', None, 'slab')
The draws below stay inside these ranges and needn't reach their ends.
Inputs may be any that keep to these rules, and one draw needn't show every extreme that they name: `block_owner`: each slot holds exactly one block. `candidate_of_group`: each candidate appears exactly once.
All inputs are finite; a program needn't handle non-finite values.
Results may differ from the reference program's by a relative error of at most 0.0003.
Values sent between devices are 32-bit elements; how exact they have to be, the bound alone decides.
A program may use at most 64 MiB of HBM per device.

```python
import math
import jax
import jax.numpy as jnp
from jax import lax

NY = 32
NZ = 128
STEPS = 8
NX = 32
CANDIDATES = 16
N_CAND = 4


def block_levels(rng, extent, shards, least, high):
    def one(axis_at, blocks):
        draws = jax.random.uniform(jax.random.fold_in(jax.random.fold_in(rng, 6), axis_at), (blocks,), jnp.float32, least / len(shards), high / len(shards))
        return jnp.repeat(jnp.exp(draws), extent[axis_at] // blocks).reshape((-1,) + (1,) * (len(extent) - axis_at - 1))

    level = one(*shards[0])
    for cut in shards[1:]:
        level = level * one(*cut)
    return level


def centred(stream_key, extent, deviation, limit, pieces=(), held_as=jnp.bfloat16):
    factor_of = block_levels(stream_key, extent, pieces, -0.22, 0.18) if pieces else 1.0
    entries = jax.random.normal(stream_key, extent, jnp.float32) * deviation * factor_of
    return jnp.minimum(jnp.maximum(entries, -limit), limit).astype(held_as)


def setup_inputs(seed: int = 0) -> dict:
    splits = jax.random.split(jax.random.key(seed), 10)
    velocity = centred(splits[0], (3, NX, NY, NZ), 1.0, 6.0, ((1, 8),), jnp.float32)
    stress = centred(splits[1], (6, NX, NY, NZ), 1.0, 6.0, ((1, 8),), jnp.float32)
    lame_lambda = jnp.clip(jnp.exp(math.log(1.5) - 1.0986123 * jax.random.uniform(splits[2], (NX, NY, NZ), jnp.float32) ** block_levels(splits[2], (NX, NY, NZ), ((0, 8),), -0.2, 0.2)), 0.5, 1.5).astype(jnp.bfloat16)
    shear_modulus = jnp.clip(jnp.exp(math.log(1.0) - 1.2078867 * jax.random.uniform(splits[3], (NX, NY, NZ), jnp.float32) ** block_levels(splits[3], (NX, NY, NZ), ((0, 8),), -0.2, 0.2)), 0.29882812, 1.0).astype(jnp.bfloat16)
    buoyancy = jnp.clip(jnp.exp(math.log(1.5) - 1.0986123 * jax.random.uniform(splits[4], (NX, NY, NZ), jnp.float32) ** block_levels(splits[4], (NX, NY, NZ), ((0, 8),), -0.2, 0.2)), 0.5, 1.5).astype(jnp.bfloat16)
    surface = centred(splits[5], (STEPS, 6, NX, NY), 1.0, 6.0, ((2, 8), (3, 4)), jnp.float32)
    block_owner = jax.random.permutation(splits[6], N_CAND).astype(jnp.int32)
    candidates = jnp.clip(jnp.exp(jax.random.uniform(splits[7], (CANDIDATES, 3), jnp.float32, math.log(0.7), math.log(1.4))), 0.7, 1.4)
    candidate_of_group = jax.random.permutation(splits[8], CANDIDATES).astype(jnp.int32)
    return {"velocity": velocity, "stress": stress, "lame_lambda": lame_lambda, "shear_modulus": shear_modulus, "buoyancy": buoyancy, "surface": surface, "block_owner": block_owner, "candidates": candidates, "candidate_of_group": candidate_of_group}


DT = 0.15


def minus_x(field, lower):
    return field - jnp.concatenate([lower[None], field[:-1]], axis=0)


def plus_x(field, upper):
    return jnp.concatenate([field[1:], upper[None]], axis=0) - field


def minus_y(field):
    edge = jnp.zeros_like(field[..., :1, :])
    return field - jnp.concatenate([edge, field[..., :-1, :]], axis=-2)


def plus_y(field):
    edge = jnp.zeros_like(field[..., :1, :])
    return jnp.concatenate([field[..., 1:, :], edge], axis=-2) - field


def minus_z(field):
    edge = jnp.zeros_like(field[..., :1])
    return field - jnp.concatenate([edge, field[..., :-1]], axis=-1)


def plus_z(field):
    edge = jnp.zeros_like(field[..., :1])
    return jnp.concatenate([field[..., 1:], edge], axis=-1) - field


def advance_velocity(vel, sig, lower, buoy, inject, zmask):
    acc_x = minus_x(sig[0], lower[0]) + minus_y(sig[3]) + minus_z(sig[4]) + inject[0][..., None] * zmask
    acc_y = minus_x(sig[3], lower[1]) + minus_y(sig[1]) + minus_z(sig[5]) + inject[1][..., None] * zmask
    acc_z = minus_x(sig[4], lower[2]) + minus_y(sig[5]) + minus_z(sig[2]) + inject[2][..., None] * zmask
    return vel + DT * buoy * jnp.stack([acc_x, acc_y, acc_z])


def advance_stress(sig, vel, upper, lam, shear, inject, zmask):
    strain_xx = plus_x(vel[0], upper[0])
    strain_yy = plus_y(vel[1])
    strain_zz = plus_z(vel[2])
    spread = strain_xx + strain_yy + strain_zz
    new_xx = sig[0] + DT * (lam * spread + 2.0 * shear * strain_xx)
    new_yy = sig[1] + DT * (lam * spread + 2.0 * shear * strain_yy)
    new_zz = sig[2] + DT * (lam * spread + 2.0 * shear * strain_zz + (lam + 2.0 * shear) * (inject[2][..., None] * zmask))
    new_xy = sig[3] + DT * shear * (plus_y(vel[0]) + plus_x(vel[1], upper[1]))
    new_xz = sig[4] + DT * shear * (plus_z(vel[0]) + plus_x(vel[2], upper[2]) + inject[0][..., None] * zmask)
    new_yz = sig[5] + DT * shear * (plus_z(vel[1]) + plus_y(vel[2]) + inject[1][..., None] * zmask)
    return jnp.stack([new_xx, new_yy, new_zz, new_xy, new_xz, new_yz])


def evolve(velocity, stress, lame_lambda, shear_modulus, buoyancy, plane, row):
    depth = velocity.shape[-1]
    levels = jnp.arange(depth)
    zone = (levels >= depth // 2).astype(jnp.float32)
    zmask = (levels == depth // 8).astype(jnp.float32)
    lam = lame_lambda.astype(jnp.float32) * (1.0 + (row[0] - 1.0) * zone)
    shear = shear_modulus.astype(jnp.float32) * (1.0 + (row[1] - 1.0) * zone)
    buoy = buoyancy.astype(jnp.float32) * (1.0 + (row[2] - 1.0) * zone)
    border = jnp.zeros((3,) + velocity.shape[2:], jnp.float32)
    vel, sig = velocity, stress
    for step in range(plane.shape[0]):
        vel = advance_velocity(vel, sig, border, buoy, plane[step, :3], zmask)
        sig = advance_stress(sig, vel, border, lam, shear, plane[step, 3:], zmask)
    return vel, sig


def reference(velocity, stress, lame_lambda, shear_modulus, buoyancy, surface, block_owner, candidates, candidate_of_group):
    groups = block_owner.shape[0]
    shaped = surface.reshape(surface.shape[:3] + (groups, surface.shape[3] // groups))
    plane = jnp.take(shaped, block_owner, axis=3).reshape(surface.shape)

    def one_group(group):
        row = candidates[candidate_of_group[group]]
        return evolve(velocity, stress, lame_lambda, shear_modulus, buoyancy, plane, row)

    vel_all, sig_all = lax.map(one_group, jnp.arange(groups, dtype=jnp.int32))
    return vel_all, sig_all
```

```python
import functools

import jax
import jax.numpy as jnp
from jax import lax
from jax.experimental import pallas as pl
from jax.experimental.pallas import tpu as pltpu
from jax.sharding import PartitionSpec as P

DT = 0.15
MESH = pl.DeviceIdType.MESH
ABOVE = 1
BELOW = 1
TOP = 8
CHUNK = 32
CROSS = (0, 3, 4)


def kernel(
    groups,
    slabs,
    steps,
    owner_ref,
    table_ref,
    order_ref,
    vel_ref,
    sig_ref,
    lam_ref,
    mu_ref,
    buoy_ref,
    block_ref,
    vel_out,
    sig_out,
    V,
    S,
    M,
    E,
    raw,
    blocks,
    rows,
    per_step,
    down_in,
    up_in,
    down_out,
    up_out,
    vel_last,
    sig_last,
    local_sem,
    block_send,
    block_recv,
    ghost_send,
    ghost_recv,
    down_send,
    down_recv,
    up_send,
    up_recv,
    out_sem,
):
    planes, width, depth = vel_ref.shape[1:]
    n = BELOW + planes + ABOVE
    own = BELOW
    group = lax.axis_index("cand")
    slab = lax.axis_index("slab")
    has_lower = slab > 0
    has_upper = slab < slabs - 1
    lower, upper = slab - 1, slab + 1
    dplane = own + ABOVE
    uplane = own + planes - 1 - BELOW

    barrier = pltpu.get_barrier_semaphore()
    for k in range(1, groups):
        pl.semaphore_signal(
            barrier, inc=1, device_id=(lax.rem(group + k, groups), slab), device_id_type=MESH
        )

    @pl.when(has_lower)
    def _():
        for k in range(groups):
            pl.semaphore_signal(
                barrier, inc=1, device_id=(lax.rem(group + k, groups), lower), device_id_type=MESH
            )

    @pl.when(has_upper)
    def _():
        for k in range(groups):
            pl.semaphore_signal(
                barrier, inc=1, device_id=(lax.rem(group + k, groups), upper), device_id_type=MESH
            )

    loads = [
        pltpu.make_async_copy(lam_ref, raw.at[0], local_sem.at[0]),
        pltpu.make_async_copy(mu_ref, raw.at[1], local_sem.at[1]),
        pltpu.make_async_copy(buoy_ref, raw.at[2], local_sem.at[2]),
        pltpu.make_async_copy(block_ref, blocks.at[1, group], local_sem.at[3]),
        pltpu.make_async_copy(
            vel_ref, V.at[:, pl.ds(own, planes), pl.ds(0, width)], local_sem.at[4]
        ),
        pltpu.make_async_copy(
            sig_ref, S.at[:, pl.ds(own, planes), pl.ds(TOP, width)], local_sem.at[5]
        ),
    ]
    for load in loads:
        load.start()

    V[:, :, width:] = jnp.zeros((3, n, V.shape[2] - width, depth), jnp.float32)
    S[:, :, :TOP] = jnp.zeros((6, n, TOP, depth), jnp.float32)

    @pl.when(jnp.logical_not(has_lower))
    def _():
        up_in[...] = jnp.zeros_like(up_in)
        blocks[0] = jnp.zeros(blocks.shape[1:], jnp.float32)
        if BELOW:
            V[:, :BELOW, :width] = jnp.zeros((3, BELOW, width, depth), jnp.float32)
            S[:, :BELOW, TOP:] = jnp.zeros((6, BELOW, width, depth), jnp.float32)
            M[:, :BELOW] = jnp.zeros((3, BELOW, width, depth), jnp.float32)

    @pl.when(jnp.logical_not(has_upper))
    def _():
        down_in[...] = jnp.zeros_like(down_in)
        blocks[2] = jnp.zeros(blocks.shape[1:], jnp.float32)
        if ABOVE:
            V[:, n - ABOVE :, :width] = jnp.zeros((3, ABOVE, width, depth), jnp.float32)
            S[:, n - ABOVE :, TOP:] = jnp.zeros((6, ABOVE, width, depth), jnp.float32)
            M[:, n - ABOVE :] = jnp.zeros((3, ABOVE, width, depth), jnp.float32)

    lane = lax.broadcasted_iota(jnp.int32, (width, depth), 1)
    zone = lax.broadcasted_iota(jnp.int32, (planes, width, depth), 2) >= depth // 2
    chosen = order_ref[group]
    for load in loads[:3]:
        load.wait()
    for which in range(3):
        scale = jnp.where(zone, table_ref[chosen, which] * DT, DT)
        M[which, own : own + planes] = raw[which].astype(jnp.float32) * scale

    sides = has_lower.astype(jnp.int32) + has_upper.astype(jnp.int32)
    pl.semaphore_wait(barrier, groups - 1 + groups * sides)

    def block_copy(level, slot, to, index):
        return pltpu.make_async_remote_copy(
            src_ref=block_ref,
            dst_ref=blocks.at[level, slot],
            send_sem=block_send.at[level, index],
            recv_sem=block_recv.at[level, slot],
            device_id=to,
            device_id_type=MESH,
        )

    def ghost_copies(down):
        count, to = (ABOVE, lower) if down else (BELOW, upper)
        base = 0 if down else 3
        source = 0 if down else planes - BELOW
        target = own + planes if down else 0
        pairs = []
        if count:
            there = pl.ds(target, count)
            pairs = [
                (sig_ref.at[:, pl.ds(source, count)], S.at[:, there, pl.ds(TOP, width)]),
                (vel_ref.at[:, pl.ds(source, count)], V.at[:, there, pl.ds(0, width)]),
                (M.at[:, pl.ds(own + source, count)], M.at[:, there]),
            ]
        else:
            base = 3
        if not down:
            edge = planes - 1 - BELOW
            pairs.append((sig_ref.at[0, edge], up_in.at[0, 0]))
            pairs.append((sig_ref.at[pl.ds(3, 2), edge], up_in.at[0, pl.ds(1, 2)]))
        return [
            pltpu.make_async_remote_copy(
                src_ref=src,
                dst_ref=dst,
                send_sem=ghost_send.at[base + at],
                recv_sem=ghost_recv.at[base + at],
                device_id=(group, to),
                device_id_type=MESH,
            )
            for at, (src, dst) in enumerate(pairs)
        ]

    def level_slots(level):
        return range(1 if level == 1 else 0, groups)

    def send_blocks(level, to):
        for k in level_slots(level):
            block_copy(level, group, (lax.rem(group + k, groups), to), k).start()

    def each_side(low, high):
        pl.when(has_lower)(low)
        pl.when(has_upper)(high)

    send_blocks(1, slab)

    def first_low():
        send_blocks(2, lower)
        for copy in ghost_copies(True):
            copy.start()

    def first_high():
        send_blocks(0, upper)
        for copy in ghost_copies(False):
            copy.start()

    each_side(first_low, first_high)

    def take_blocks(level, to):
        for k in level_slots(level):
            slot = lax.rem(group + k, groups)
            block_copy(level, slot, (slot, to), k).wait_recv()

    loads[3].wait()
    take_blocks(1, slab)
    each_side(lambda: take_blocks(0, lower), lambda: take_blocks(2, upper))
    columns = width // groups
    for level in range(3):
        for j in range(groups):
            rows[level, j * columns : (j + 1) * columns] = blocks[level, owner_ref[j]]
    halves = 128 // CHUNK
    for t in range(steps):
        at = 128 * (t // halves)
        for level in range(3):
            piece = rows[level, :, at : at + 128]
            shift = (t % halves) * CHUNK
            per_step[t, level] = pltpu.roll(piece, 128 - shift, 1) if shift else piece

    source_level = depth // 8

    def spread(t, carry):
        for i in range(n):
            x = i - own
            level = 0 if x < 0 else 2 if x >= planes else 1
            value = per_step[t, level]
            for c in range(6):
                at = c * planes + x % planes
                moved = pltpu.roll(value, (source_level - at) % depth, 1)
                E[t, c, i] = jnp.where(lane == source_level, moved, 0.0)
        return carry

    lax.fori_loop(0, steps, spread, 0)

    for load in loads[4:]:
        load.wait()

    def ghosts_here():
        for copy in ghost_copies(True):
            copy.wait_recv()

    def ghosts_below_here():
        for copy in ghost_copies(False):
            copy.wait_recv()

    each_side(ghosts_below_here, ghosts_here)

    def before(f):
        return jnp.where(lane == 0, 0.0, pltpu.roll(f, 1, 1))

    def after(f):
        return jnp.where(lane == depth - 1, 0.0, pltpu.roll(f, depth - 1, 1))

    def here(c, i):
        return S[c, i, TOP : TOP + width]

    def south(c, i):
        return S[c, i, TOP - 1 : TOP - 1 + width]

    def new_vel(i, t):
        if i == 0:
            west = [up_in[t, c] for c in range(3)]
        else:
            west = [here(c, i - 1) for c in CROSS]
        sxx, syy, szz, sxy, sxz, syz = (here(c, i) for c in range(6))
        b = M[2, i]
        ax = (sxx - west[0]) + (sxy - south(3, i)) + (sxz - before(sxz)) + E[t, 0, i]
        ay = (sxy - west[1]) + (syy - south(1, i)) + (syz - before(syz)) + E[t, 1, i]
        az = (sxz - west[2]) + (syz - south(5, i)) + (szz - before(szz)) + E[t, 2, i]
        return [V[c, i, :width] + b * a for c, a in enumerate((ax, ay, az))]

    def new_sig(i, t):
        vx, vy, vz = (V[c, i, :width] for c in range(3))
        nx, ny, nz = (V[c, i, 1 : 1 + width] for c in range(3))
        if i == n - 1:
            ex, ey, ez = (down_in[t, c] for c in range(3))
        else:
            ex, ey, ez = (V[c, i + 1, :width] for c in range(3))
        lam, mu = M[0, i], M[1, i]
        mu2 = mu + mu
        xx, yy, zz = ex - vx, ny - vy, after(vz) - vz
        zz_in = E[t, 5, i]
        spread_all = lam * (xx + yy + zz)
        return [
            here(0, i) + (spread_all + mu2 * xx),
            here(1, i) + (spread_all + mu2 * yy),
            here(2, i) + (spread_all + mu2 * zz + (lam + mu2) * zz_in),
            here(3, i) + mu * ((nx - vx) + (ey - vy)),
            here(4, i) + mu * ((after(vx) - vx) + (ez - vz) + E[t, 3, i]),
            here(5, i) + mu * ((after(vy) - vy) + (nz - vz) + E[t, 4, i]),
        ]

    def set_vel(i, t):
        values = new_vel(i, t)
        for c in range(3):
            V[c, i, :width] = values[c]
        return values

    def set_sig(i, t):
        values = new_sig(i, t)
        for c in range(6):
            S[c, i, TOP : TOP + width] = values[c]
        return values

    def down_copy(t):
        return pltpu.make_async_remote_copy(
            src_ref=down_out.at[t],
            dst_ref=down_in.at[t],
            send_sem=down_send.at[t],
            recv_sem=down_recv.at[t],
            device_id=(group, lower),
            device_id_type=MESH,
        )

    def up_copy(t):
        return pltpu.make_async_remote_copy(
            src_ref=up_out.at[t],
            dst_ref=up_in.at[t + 1],
            send_sem=up_send.at[t],
            recv_sem=up_recv.at[t],
            device_id=(group, upper),
            device_id_type=MESH,
        )

    last_up = steps - 2 - BELOW

    def finish_top(t):
        @pl.when(has_upper)
        def _():
            down_copy(t - 1).wait_recv()

        set_sig(n - 1, t - 1)

    def send_up(t):
        values = set_sig(uplane, t)

        @pl.when(jnp.logical_and(has_upper, t <= last_up))
        def _():
            for at, c in enumerate(CROSS):
                up_out[t, at] = values[c]
            up_copy(t).start()

    def one_step(t, carry):
        values = set_vel(dplane, t)

        @pl.when(has_lower)
        def _():
            for c in range(3):
                down_out[t, c] = values[c]
            down_copy(t).start()

        done = [dplane]
        early = uplane + 1 <= n - 2
        if early:
            for i in (uplane, uplane + 1):
                if i not in done and i > 0:
                    set_vel(i, t)
                    done.append(i)
            send_up(t)
        for i in range(1, n - 1):
            if i not in done:
                set_vel(i, t)

        @pl.when(t > 0)
        def _():
            finish_top(t)

        set_vel(n - 1, t)
        if not early:
            send_up(t)
        for i in range(n - 2, 0, -1):
            if i != uplane:
                set_sig(i, t)

        @pl.when(jnp.logical_and(has_lower, t > 0))
        def _():
            up_copy(t - 1).wait_recv()

        set_vel(0, t)
        set_sig(0, t)
        return carry

    lax.fori_loop(0, steps - 1, one_step, 0)

    t = steps - 1
    out_copies = []

    def store(ref, out, i, values, sem):
        x = i - own
        for c, value in enumerate(values):
            ref[c, x] = value
        copy = pltpu.make_async_copy(ref.at[:, x], out.at[0, :, x], out_sem.at[sem, x])
        copy.start()
        out_copies.append(copy)

    if BELOW == 0:

        @pl.when(has_lower)
        def _():
            up_copy(t - 1).wait_recv()

    for i in range(own, own + planes):
        values = set_vel(i, t)
        store(vel_last, vel_out, i, values, 0)
    for i in range(own, own + planes - 1):
        store(sig_last, sig_out, i, new_sig(i, t), 1)
    finish_top(t)
    set_vel(own + planes, t)
    i = own + planes - 1
    store(sig_last, sig_out, i, new_sig(i, t), 1)

    for k in level_slots(1):
        block_copy(1, group, (lax.rem(group + k, groups), slab), k).wait_send()

    def sent_low():
        for k in level_slots(2):
            block_copy(2, group, (lax.rem(group + k, groups), lower), k).wait_send()
        for copy in ghost_copies(True):
            copy.wait_send()
        for s in range(steps - 1):
            down_copy(s).wait_send()

    def sent_high():
        for k in level_slots(0):
            block_copy(0, group, (lax.rem(group + k, groups), upper), k).wait_send()
        for copy in ghost_copies(False):
            copy.wait_send()
        for s in range(last_up + 1):
            up_copy(s).wait_send()

    each_side(sent_low, sent_high)
    for copy in out_copies:
        copy.wait()


def body(
    groups,
    slabs,
    velocity,
    stress,
    lame_lambda,
    shear_modulus,
    buoyancy,
    surface,
    block_owner,
    candidates,
    candidate_of_group,
):
    planes, width, depth = velocity.shape[1:]
    steps, parts = surface.shape[:2]
    columns = surface.shape[3]
    n = BELOW + planes + ABOVE
    packed = surface.transpose(3, 0, 1, 2).reshape(columns, steps, parts * planes)
    packed = jnp.pad(packed, ((0, 0), (0, 0), (0, CHUNK - parts * planes)))
    packed = packed.reshape(columns, steps * CHUNK)
    lanes = steps * CHUNK
    any_space = pl.BlockSpec(memory_space=pl.ANY)
    scalars = pl.BlockSpec(memory_space=pltpu.SMEM)
    f32 = jnp.float32
    message = pltpu.VMEM((steps, 3, width, depth), f32)
    dma = pltpu.SemaphoreType.DMA
    return pl.pallas_call(
        functools.partial(kernel, groups, slabs, steps),
        out_shape=(
            jax.ShapeDtypeStruct((1, 3, planes, width, depth), f32),
            jax.ShapeDtypeStruct((1, 6, planes, width, depth), f32),
        ),
        in_specs=[scalars] * 3 + [any_space] * 6,
        out_specs=(any_space, any_space),
        scratch_shapes=[
            pltpu.VMEM((3, n, width + 8, depth), f32),
            pltpu.VMEM((6, n, width + TOP, depth), f32),
            pltpu.VMEM((3, n, width, depth), f32),
            pltpu.VMEM((steps, 6, n, width, depth), f32),
            pltpu.VMEM((3, planes, width, depth), jnp.bfloat16),
            pltpu.VMEM((3, groups, columns, lanes), f32),
            pltpu.VMEM((3, width, lanes), f32),
            pltpu.VMEM((steps, 3, width, 128), f32),
            message,
            message,
            message,
            message,
            pltpu.VMEM((3, planes, width, depth), f32),
            pltpu.VMEM((6, planes, width, depth), f32),
            dma((6,)),
            dma((3, groups)),
            dma((3, groups)),
            dma((8,)),
            dma((8,)),
            dma((steps,)),
            dma((steps,)),
            dma((steps,)),
            dma((steps,)),
            dma((2, planes)),
        ],
        compiler_params=pltpu.CompilerParams(
            collective_id=0, has_side_effects=True, vmem_limit_bytes=40 * 1024 * 1024
        ),
    )(
        block_owner,
        candidates,
        candidate_of_group,
        velocity,
        stress,
        lame_lambda,
        shear_modulus,
        buoyancy,
        packed,
    )


def solution(mesh):
    in_specs = (
        P(None, "slab", None, None),
        P(None, "slab", None, None),
        P("slab", None, None),
        P("slab", None, None),
        P("slab", None, None),
        P(None, None, "slab", "cand"),
        P(),
        P(),
        P(),
    )
    out_specs = (P("cand", None, "slab", None, None), P("cand", None, "slab", None, None))
    return jax.shard_map(
        functools.partial(body, mesh.shape["cand"], mesh.shape["slab"]),
        mesh=mesh,
        in_specs=in_specs,
        out_specs=out_specs,
        check_vma=False,
    )
```

```python
import functools

import jax
import jax.numpy as jnp
from jax import lax
from jax.experimental import pallas as pl
from jax.experimental.pallas import tpu as pltpu
from jax.sharding import PartitionSpec as P

DT = 0.15
VMEM = 62 * 1024 * 1024
MESH = pl.DeviceIdType.MESH
ABOVE = 1
BELOW = 1
TOP = 8
CHUNK = 32
CROSS = (0, 3, 4)


def kernel(
    groups,
    slabs,
    steps,
    owner_ref,
    table_ref,
    order_ref,
    vel_ref,
    sig_ref,
    lam_ref,
    mu_ref,
    buoy_ref,
    surface_ref,
    vel_out,
    sig_out,
    V,
    S,
    M,
    E,
    raw,
    raw_rows,
    tall,
    packed,
    blocks,
    rows,
    per_step,
    down_in,
    up_in,
    down_out,
    up_out,
    vel_last,
    sig_last,
    local_sem,
    block_send,
    block_recv,
    ghost_send,
    ghost_recv,
    down_send,
    down_recv,
    up_send,
    up_recv,
    out_sem,
):
    planes, width, depth = vel_ref.shape[1:]
    n = BELOW + planes + ABOVE
    own = BELOW
    group = lax.axis_index("cand")
    slab = lax.axis_index("slab")
    has_lower = slab > 0
    has_upper = slab < slabs - 1
    lower, upper = slab - 1, slab + 1
    dplane = own + ABOVE
    uplane = own + planes - 1 - BELOW

    barrier = pltpu.get_barrier_semaphore()
    for k in range(1, groups):
        pl.semaphore_signal(
            barrier, inc=1, device_id=(lax.rem(group + k, groups), slab), device_id_type=MESH
        )

    @pl.when(has_lower)
    def _():
        for k in range(groups):
            pl.semaphore_signal(
                barrier, inc=1, device_id=(lax.rem(group + k, groups), lower), device_id_type=MESH
            )

    @pl.when(has_upper)
    def _():
        for k in range(groups):
            pl.semaphore_signal(
                barrier, inc=1, device_id=(lax.rem(group + k, groups), upper), device_id_type=MESH
            )

    parts = surface_ref.shape[0] // steps
    columns = width // groups
    loads = [
        pltpu.make_async_copy(lam_ref, raw.at[0], local_sem.at[0]),
        pltpu.make_async_copy(mu_ref, raw.at[1], local_sem.at[1]),
        pltpu.make_async_copy(buoy_ref, raw.at[2], local_sem.at[2]),
        pltpu.make_async_copy(surface_ref, raw_rows, local_sem.at[3]),
        pltpu.make_async_copy(
            vel_ref, V.at[:, pl.ds(own, planes), pl.ds(0, width)], local_sem.at[4]
        ),
        pltpu.make_async_copy(
            sig_ref, S.at[:, pl.ds(own, planes), pl.ds(TOP, width)], local_sem.at[5]
        ),
    ]
    for load in loads:
        load.start()

    V[:, :, width:] = jnp.zeros((3, n, V.shape[2] - width, depth), jnp.float32)
    S[:, :, :TOP] = jnp.zeros((6, n, TOP, depth), jnp.float32)

    @pl.when(jnp.logical_not(has_lower))
    def _():
        up_in[...] = jnp.zeros_like(up_in)
        blocks[0] = jnp.zeros(blocks.shape[1:], jnp.float32)
        if BELOW:
            V[:, :BELOW, :width] = jnp.zeros((3, BELOW, width, depth), jnp.float32)
            S[:, :BELOW, TOP:] = jnp.zeros((6, BELOW, width, depth), jnp.float32)
            M[:, :BELOW] = jnp.zeros((3, BELOW, width, depth), jnp.float32)

    @pl.when(jnp.logical_not(has_upper))
    def _():
        down_in[...] = jnp.zeros_like(down_in)
        blocks[2] = jnp.zeros(blocks.shape[1:], jnp.float32)
        if ABOVE:
            V[:, n - ABOVE :, :width] = jnp.zeros((3, ABOVE, width, depth), jnp.float32)
            S[:, n - ABOVE :, TOP:] = jnp.zeros((6, ABOVE, width, depth), jnp.float32)
            M[:, n - ABOVE :] = jnp.zeros((3, ABOVE, width, depth), jnp.float32)

    tall[...] = jnp.zeros_like(tall)
    loads[3].wait()
    for t in range(steps):
        for c in range(parts):
            at = t * CHUNK + c * planes
            tall[at : at + planes, :columns] = raw_rows[t * parts + c]
    for at in range(0, steps * CHUNK, 128):
        turned = tall[at : at + 128, :].T[:columns]
        packed[:, at : at + 128] = turned
        blocks[1, group, :, at : at + 128] = turned

    lane = lax.broadcasted_iota(jnp.int32, (width, depth), 1)
    zone = lax.broadcasted_iota(jnp.int32, (planes, width, depth), 2) >= depth // 2
    chosen = order_ref[group]
    for load in loads[:3]:
        load.wait()
    for which in range(3):
        scale = jnp.where(zone, table_ref[which, chosen] * DT, DT)
        M[which, own : own + planes] = raw[which].astype(jnp.float32) * scale

    sides = has_lower.astype(jnp.int32) + has_upper.astype(jnp.int32)
    pl.semaphore_wait(barrier, groups - 1 + groups * sides)

    def block_copy(level, slot, to, index):
        return pltpu.make_async_remote_copy(
            src_ref=packed,
            dst_ref=blocks.at[level, slot],
            send_sem=block_send.at[level, index],
            recv_sem=block_recv.at[level, slot],
            device_id=to,
            device_id_type=MESH,
        )

    def ghost_copies(down):
        count, to = (ABOVE, lower) if down else (BELOW, upper)
        base = 0 if down else 3
        source = 0 if down else planes - BELOW
        target = own + planes if down else 0
        pairs = []
        if count:
            there = pl.ds(target, count)
            pairs = [
                (sig_ref.at[:, pl.ds(source, count)], S.at[:, there, pl.ds(TOP, width)]),
                (vel_ref.at[:, pl.ds(source, count)], V.at[:, there, pl.ds(0, width)]),
                (M.at[:, pl.ds(own + source, count)], M.at[:, there]),
            ]
        else:
            base = 3
        if not down:
            edge = planes - 1 - BELOW
            pairs.append((sig_ref.at[0, edge], up_in.at[0, 0]))
            pairs.append((sig_ref.at[pl.ds(3, 2), edge], up_in.at[0, pl.ds(1, 2)]))
        return [
            pltpu.make_async_remote_copy(
                src_ref=src,
                dst_ref=dst,
                send_sem=ghost_send.at[base + at],
                recv_sem=ghost_recv.at[base + at],
                device_id=(group, to),
                device_id_type=MESH,
            )
            for at, (src, dst) in enumerate(pairs)
        ]

    def level_slots(level):
        return range(1 if level == 1 else 0, groups)

    def send_blocks(level, to):
        for k in level_slots(level):
            block_copy(level, group, (lax.rem(group + k, groups), to), k).start()

    def each_side(low, high):
        pl.when(has_lower)(low)
        pl.when(has_upper)(high)

    send_blocks(1, slab)

    def first_low():
        send_blocks(2, lower)
        for copy in ghost_copies(True):
            copy.start()

    def first_high():
        send_blocks(0, upper)
        for copy in ghost_copies(False):
            copy.start()

    each_side(first_low, first_high)

    def take_blocks(level, to):
        for k in level_slots(level):
            slot = lax.rem(group + k, groups)
            block_copy(level, slot, (slot, to), k).wait_recv()

    take_blocks(1, slab)
    each_side(lambda: take_blocks(0, lower), lambda: take_blocks(2, upper))
    for level in range(3):
        for j in range(groups):
            rows[level, j * columns : (j + 1) * columns] = blocks[level, owner_ref[j]]
    halves = 128 // CHUNK
    for t in range(steps):
        at = 128 * (t // halves)
        for level in range(3):
            piece = rows[level, :, at : at + 128]
            shift = (t % halves) * CHUNK
            per_step[t, level] = pltpu.roll(piece, 128 - shift, 1) if shift else piece

    source_level = depth // 8

    def spread(t, carry):
        for i in range(n):
            x = i - own
            level = 0 if x < 0 else 2 if x >= planes else 1
            value = per_step[t, level]
            for c in range(parts):
                at = c * planes + x % planes
                moved = pltpu.roll(value, (source_level - at) % depth, 1)
                E[t, c, i] = jnp.where(lane == source_level, moved, 0.0)
        return carry

    lax.fori_loop(0, steps, spread, 0)

    for load in loads[4:]:
        load.wait()

    def ghosts_here():
        for copy in ghost_copies(True):
            copy.wait_recv()

    def ghosts_below_here():
        for copy in ghost_copies(False):
            copy.wait_recv()

    each_side(ghosts_below_here, ghosts_here)

    def before(f):
        return jnp.where(lane == 0, 0.0, pltpu.roll(f, 1, 1))

    def after(f):
        return jnp.where(lane == depth - 1, 0.0, pltpu.roll(f, depth - 1, 1))

    def here(c, i):
        return S[c, i, TOP : TOP + width]

    def south(c, i):
        return S[c, i, TOP - 1 : TOP - 1 + width]

    def new_vel(i, t):
        if i == 0:
            west = [up_in[t, c] for c in range(3)]
        else:
            west = [here(c, i - 1) for c in CROSS]
        sxx, syy, szz, sxy, sxz, syz = (here(c, i) for c in range(6))
        b = M[2, i]
        ax = (sxx - west[0]) + (sxy - south(3, i)) + (sxz - before(sxz)) + E[t, 0, i]
        ay = (sxy - west[1]) + (syy - south(1, i)) + (syz - before(syz)) + E[t, 1, i]
        az = (sxz - west[2]) + (syz - south(5, i)) + (szz - before(szz)) + E[t, 2, i]
        return [V[c, i, :width] + b * a for c, a in enumerate((ax, ay, az))]

    def new_sig(i, t):
        vx, vy, vz = (V[c, i, :width] for c in range(3))
        nx, ny, nz = (V[c, i, 1 : 1 + width] for c in range(3))
        if i == n - 1:
            ex, ey, ez = (down_in[t, c] for c in range(3))
        else:
            ex, ey, ez = (V[c, i + 1, :width] for c in range(3))
        lam, mu = M[0, i], M[1, i]
        mu2 = mu + mu
        xx, yy, zz = ex - vx, ny - vy, after(vz) - vz
        zz_in = E[t, 5, i]
        spread_all = lam * (xx + yy + zz)
        return [
            here(0, i) + (spread_all + mu2 * xx),
            here(1, i) + (spread_all + mu2 * yy),
            here(2, i) + (spread_all + mu2 * zz + (lam + mu2) * zz_in),
            here(3, i) + mu * ((nx - vx) + (ey - vy)),
            here(4, i) + mu * ((after(vx) - vx) + (ez - vz) + E[t, 3, i]),
            here(5, i) + mu * ((after(vy) - vy) + (nz - vz) + E[t, 4, i]),
        ]

    def set_vel(i, t):
        values = new_vel(i, t)
        for c in range(3):
            V[c, i, :width] = values[c]
        return values

    def set_sig(i, t):
        values = new_sig(i, t)
        for c in range(6):
            S[c, i, TOP : TOP + width] = values[c]
        return values

    def down_copy(t):
        return pltpu.make_async_remote_copy(
            src_ref=down_out.at[t],
            dst_ref=down_in.at[t],
            send_sem=down_send.at[t],
            recv_sem=down_recv.at[t],
            device_id=(group, lower),
            device_id_type=MESH,
        )

    def up_copy(t):
        return pltpu.make_async_remote_copy(
            src_ref=up_out.at[t],
            dst_ref=up_in.at[t + 1],
            send_sem=up_send.at[t],
            recv_sem=up_recv.at[t],
            device_id=(group, upper),
            device_id_type=MESH,
        )

    last_up = steps - 2 - BELOW

    def finish_top(t):
        @pl.when(has_upper)
        def _():
            down_copy(t - 1).wait_recv()

        set_sig(n - 1, t - 1)

    def send_up(t):
        values = set_sig(uplane, t)

        @pl.when(jnp.logical_and(has_upper, t <= last_up))
        def _():
            for at, c in enumerate(CROSS):
                up_out[t, at] = values[c]
            up_copy(t).start()

    def one_step(t, carry):
        values = set_vel(dplane, t)

        @pl.when(has_lower)
        def _():
            for c in range(3):
                down_out[t, c] = values[c]
            down_copy(t).start()

        done = [dplane]
        early = uplane + 1 <= n - 2
        if early:
            for i in (uplane, uplane + 1):
                if i not in done and i > 0:
                    set_vel(i, t)
                    done.append(i)
            send_up(t)
        for i in range(1, n - 1):
            if i not in done:
                set_vel(i, t)

        @pl.when(t > 0)
        def _():
            finish_top(t)

        set_vel(n - 1, t)
        if not early:
            send_up(t)
        for i in range(n - 2, 0, -1):
            if i != uplane:
                set_sig(i, t)

        @pl.when(jnp.logical_and(has_lower, t > 0))
        def _():
            up_copy(t - 1).wait_recv()

        set_vel(0, t)
        set_sig(0, t)
        return carry

    lax.fori_loop(0, steps - 1, one_step, 0)

    t = steps - 1

    out_copies = []

    def store(ref, out, i, values, kind):
        x = i - own
        for c, value in enumerate(values):
            ref[c, x] = value
        copy = pltpu.make_async_copy(ref.at[:, x], out.at[0, :, x], out_sem.at[kind, x])
        copy.start()
        out_copies.append(copy)

    if BELOW == 0:

        @pl.when(has_lower)
        def _():
            up_copy(t - 1).wait_recv()

    for i in range(own, own + planes):
        values = set_vel(i, t)
        store(vel_last, vel_out, i, values, 0)
    for i in range(own, own + planes - 1):
        store(sig_last, sig_out, i, new_sig(i, t), 1)
    finish_top(t)
    set_vel(own + planes, t)
    i = own + planes - 1
    store(sig_last, sig_out, i, new_sig(i, t), 1)

    for k in level_slots(1):
        block_copy(1, group, (lax.rem(group + k, groups), slab), k).wait_send()

    def sent_low():
        for k in level_slots(2):
            block_copy(2, group, (lax.rem(group + k, groups), lower), k).wait_send()
        for copy in ghost_copies(True):
            copy.wait_send()
        for s in range(steps - 1):
            down_copy(s).wait_send()

    def sent_high():
        for k in level_slots(0):
            block_copy(0, group, (lax.rem(group + k, groups), upper), k).wait_send()
        for copy in ghost_copies(False):
            copy.wait_send()
        for s in range(last_up + 1):
            up_copy(s).wait_send()

    each_side(sent_low, sent_high)
    for copy in out_copies:
        copy.wait()


def hand_over(vel_ref, sig_ref, vel_out, sig_out, sem):
    pairs = [(vel_ref, vel_out, c) for c in range(3)] + [(sig_ref, sig_out, c) for c in range(6)]
    copies = [
        pltpu.make_async_copy(src.at[0, c], dst.at[0, c], sem.at[at])
        for at, (src, dst, c) in enumerate(pairs)
    ]
    for copy in copies:
        copy.start()
    for copy in copies:
        copy.wait()


def body(
    groups,
    slabs,
    velocity,
    stress,
    lame_lambda,
    shear_modulus,
    buoyancy,
    surface,
    block_owner,
    candidates,
    candidate_of_group,
):
    planes, width, depth = velocity.shape[1:]
    steps, parts = surface.shape[:2]
    columns = surface.shape[3]
    n = BELOW + planes + ABOVE
    lanes = steps * CHUNK
    far = pl.BlockSpec(memory_space=pl.ANY)
    scalars = pl.BlockSpec(memory_space=pltpu.SMEM)
    f32 = jnp.float32
    message = pltpu.VMEM((steps, 3, width, depth), f32)
    dma = pltpu.SemaphoreType.DMA
    shapes = (
        jax.ShapeDtypeStruct((1, 3, planes, width, depth), f32),
        jax.ShapeDtypeStruct((1, 6, planes, width, depth), f32),
    )
    vel, sig = pl.pallas_call(
        functools.partial(kernel, groups, slabs, steps),
        out_shape=shapes,
        in_specs=[scalars] * 3 + [far] * 6,
        out_specs=(far, far),
        scratch_shapes=[
            pltpu.VMEM((3, n, width + 8, depth), f32),
            pltpu.VMEM((6, n, width + TOP, depth), f32),
            pltpu.VMEM((3, n, width, depth), f32),
            pltpu.VMEM((steps, 6, n, width, depth), f32),
            pltpu.VMEM((3, planes, width, depth), jnp.bfloat16),
            pltpu.VMEM((steps * parts, planes, columns), f32),
            pltpu.VMEM((lanes, 128), f32),
            pltpu.VMEM((columns, lanes), f32),
            pltpu.VMEM((3, groups, columns, lanes), f32),
            pltpu.VMEM((3, width, lanes), f32),
            pltpu.VMEM((steps, 3, width, 128), f32),
            message,
            message,
            message,
            message,
            pltpu.VMEM((3, planes, width, depth), f32),
            pltpu.VMEM((6, planes, width, depth), f32),
            dma((6,)),
            dma((3, groups)),
            dma((3, groups)),
            dma((8,)),
            dma((8,)),
            dma((steps,)),
            dma((steps,)),
            dma((steps,)),
            dma((steps,)),
            dma((2, planes)),
        ],
        compiler_params=pltpu.CompilerParams(
            collective_id=0, has_side_effects=True, vmem_limit_bytes=VMEM
        ),
    )(
        block_owner,
        candidates.T,
        candidate_of_group,
        velocity,
        stress,
        lame_lambda,
        shear_modulus,
        buoyancy,
        surface.reshape(steps * parts, planes, columns),
    )
    return pl.pallas_call(
        hand_over,
        out_shape=shapes,
        in_specs=[far, far],
        out_specs=(far, far),
        scratch_shapes=[dma((9,))],
        compiler_params=pltpu.CompilerParams(vmem_limit_bytes=VMEM),
    )(vel, sig)


def solution(mesh):
    in_specs = (
        P(None, "slab", None, None),
        P(None, "slab", None, None),
        P("slab", None, None),
        P("slab", None, None),
        P("slab", None, None),
        P(None, None, "slab", "cand"),
        P(),
        P(),
        P(),
    )
    out_specs = (P("cand", None, "slab", None, None), P("cand", None, "slab", None, None))
    return jax.shard_map(
        functools.partial(body, mesh.shape["cand"], mesh.shape["slab"]),
        mesh=mesh,
        in_specs=in_specs,
        out_specs=out_specs,
        check_vma=False,
    )
```

```python
import functools

import jax
import jax.numpy as jnp
from jax import lax
from jax.experimental import pallas as pl
from jax.experimental.pallas import tpu as pltpu
from jax.sharding import PartitionSpec as P

DT = 0.15
VMEM = 62 * 1024 * 1024
MESH = pl.DeviceIdType.MESH
ABOVE = 1
BELOW = 0
TOP = 8
CHUNK = 32
CROSS = (0, 3, 4)


def kernel(
    groups,
    slabs,
    steps,
    owner_ref,
    table_ref,
    order_ref,
    vel_ref,
    sig_ref,
    lam_ref,
    mu_ref,
    buoy_ref,
    surface_ref,
    vel_out,
    sig_out,
    V,
    S,
    M,
    E,
    raw,
    raw_rows,
    tall,
    packed,
    blocks,
    rows,
    per_step,
    down_in,
    up_in,
    down_out,
    up_out,
    vel_last,
    sig_last,
    local_sem,
    block_send,
    block_recv,
    ghost_send,
    ghost_recv,
    down_send,
    down_recv,
    up_send,
    up_recv,
    out_sem,
):
    planes, width, depth = vel_ref.shape[1:]
    n = BELOW + planes + ABOVE
    own = BELOW
    group = lax.axis_index("cand")
    slab = lax.axis_index("slab")
    has_lower = slab > 0
    has_upper = slab < slabs - 1
    lower, upper = slab - 1, slab + 1
    dplane = own + ABOVE
    uplane = own + planes - 1 - BELOW

    barrier = pltpu.get_barrier_semaphore()
    for k in range(1, groups):
        pl.semaphore_signal(
            barrier, inc=1, device_id=(lax.rem(group + k, groups), slab), device_id_type=MESH
        )

    @pl.when(has_lower)
    def _():
        for k in range(groups):
            pl.semaphore_signal(
                barrier, inc=1, device_id=(lax.rem(group + k, groups), lower), device_id_type=MESH
            )

    @pl.when(has_upper)
    def _():
        for k in range(groups):
            pl.semaphore_signal(
                barrier, inc=1, device_id=(lax.rem(group + k, groups), upper), device_id_type=MESH
            )

    parts = surface_ref.shape[0] // steps
    columns = width // groups
    loads = [
        pltpu.make_async_copy(lam_ref, raw.at[0], local_sem.at[0]),
        pltpu.make_async_copy(mu_ref, raw.at[1], local_sem.at[1]),
        pltpu.make_async_copy(buoy_ref, raw.at[2], local_sem.at[2]),
        pltpu.make_async_copy(surface_ref, raw_rows, local_sem.at[3]),
        pltpu.make_async_copy(
            vel_ref, V.at[:, pl.ds(own, planes), pl.ds(0, width)], local_sem.at[4]
        ),
        pltpu.make_async_copy(
            sig_ref, S.at[:, pl.ds(own, planes), pl.ds(TOP, width)], local_sem.at[5]
        ),
    ]
    for load in loads:
        load.start()

    V[:, :, width:] = jnp.zeros((3, n, V.shape[2] - width, depth), jnp.float32)
    S[:, :, :TOP] = jnp.zeros((6, n, TOP, depth), jnp.float32)

    @pl.when(jnp.logical_not(has_lower))
    def _():
        up_in[...] = jnp.zeros_like(up_in)
        blocks[0] = jnp.zeros(blocks.shape[1:], jnp.float32)
        if BELOW:
            V[:, :BELOW, :width] = jnp.zeros((3, BELOW, width, depth), jnp.float32)
            S[:, :BELOW, TOP:] = jnp.zeros((6, BELOW, width, depth), jnp.float32)
            M[:, :BELOW] = jnp.zeros((3, BELOW, width, depth), jnp.float32)

    @pl.when(jnp.logical_not(has_upper))
    def _():
        down_in[...] = jnp.zeros_like(down_in)
        blocks[2] = jnp.zeros(blocks.shape[1:], jnp.float32)
        if ABOVE:
            V[:, n - ABOVE :, :width] = jnp.zeros((3, ABOVE, width, depth), jnp.float32)
            S[:, n - ABOVE :, TOP:] = jnp.zeros((6, ABOVE, width, depth), jnp.float32)
            M[:, n - ABOVE :] = jnp.zeros((3, ABOVE, width, depth), jnp.float32)

    tall[...] = jnp.zeros_like(tall)
    loads[3].wait()
    for t in range(steps):
        for c in range(parts):
            at = t * CHUNK + c * planes
            tall[at : at + planes, :columns] = raw_rows[t * parts + c]
    for at in range(0, steps * CHUNK, 128):
        turned = tall[at : at + 128, :].T[:columns]
        packed[:, at : at + 128] = turned
        blocks[1, group, :, at : at + 128] = turned

    lane = lax.broadcasted_iota(jnp.int32, (width, depth), 1)
    zone = lax.broadcasted_iota(jnp.int32, (planes, width, depth), 2) >= depth // 2
    chosen = order_ref[group]
    for load in loads[:3]:
        load.wait()
    for which in range(3):
        scale = jnp.where(zone, table_ref[which, chosen] * DT, DT)
        M[which, own : own + planes] = raw[which].astype(jnp.float32) * scale

    sides = has_lower.astype(jnp.int32) + has_upper.astype(jnp.int32)
    pl.semaphore_wait(barrier, groups - 1 + groups * sides)

    def block_copy(level, slot, to, index):
        return pltpu.make_async_remote_copy(
            src_ref=packed,
            dst_ref=blocks.at[level, slot],
            send_sem=block_send.at[level, index],
            recv_sem=block_recv.at[level, slot],
            device_id=to,
            device_id_type=MESH,
        )

    def ghost_copies(down):
        count, to = (ABOVE, lower) if down else (BELOW, upper)
        base = 0 if down else 3
        source = 0 if down else planes - BELOW
        target = own + planes if down else 0
        pairs = []
        if count:
            there = pl.ds(target, count)
            pairs = [
                (sig_ref.at[:, pl.ds(source, count)], S.at[:, there, pl.ds(TOP, width)]),
                (vel_ref.at[:, pl.ds(source, count)], V.at[:, there, pl.ds(0, width)]),
                (M.at[:, pl.ds(own + source, count)], M.at[:, there]),
            ]
        else:
            base = 3
        if not down:
            edge = planes - 1 - BELOW
            pairs.append((sig_ref.at[0, edge], up_in.at[0, 0]))
            pairs.append((sig_ref.at[pl.ds(3, 2), edge], up_in.at[0, pl.ds(1, 2)]))
        return [
            pltpu.make_async_remote_copy(
                src_ref=src,
                dst_ref=dst,
                send_sem=ghost_send.at[base + at],
                recv_sem=ghost_recv.at[base + at],
                device_id=(group, to),
                device_id_type=MESH,
            )
            for at, (src, dst) in enumerate(pairs)
        ]

    def level_slots(level):
        return range(1 if level == 1 else 0, groups)

    def send_blocks(level, to):
        for k in level_slots(level):
            block_copy(level, group, (lax.rem(group + k, groups), to), k).start()

    def each_side(low, high):
        pl.when(has_lower)(low)
        pl.when(has_upper)(high)

    send_blocks(1, slab)

    def first_low():
        send_blocks(2, lower)
        for copy in ghost_copies(True):
            copy.start()

    def first_high():
        send_blocks(0, upper)
        for copy in ghost_copies(False):
            copy.start()

    each_side(first_low, first_high)

    def take_blocks(level, to):
        for k in level_slots(level):
            slot = lax.rem(group + k, groups)
            block_copy(level, slot, (slot, to), k).wait_recv()

    take_blocks(1, slab)
    each_side(lambda: take_blocks(0, lower), lambda: take_blocks(2, upper))
    for level in range(3):
        for j in range(groups):
            rows[level, j * columns : (j + 1) * columns] = blocks[level, owner_ref[j]]
    halves = 128 // CHUNK
    for t in range(steps):
        at = 128 * (t // halves)
        for level in range(3):
            piece = rows[level, :, at : at + 128]
            shift = (t % halves) * CHUNK
            per_step[t, level] = pltpu.roll(piece, 128 - shift, 1) if shift else piece

    source_level = depth // 8

    def spread(t, carry):
        for i in range(n):
            x = i - own
            level = 0 if x < 0 else 2 if x >= planes else 1
            value = per_step[t, level]
            for c in range(parts):
                at = c * planes + x % planes
                moved = pltpu.roll(value, (source_level - at) % depth, 1)
                E[t, c, i] = jnp.where(lane == source_level, moved, 0.0)
        return carry

    lax.fori_loop(0, steps, spread, 0)

    for load in loads[4:]:
        load.wait()

    def ghosts_here():
        for copy in ghost_copies(True):
            copy.wait_recv()

    def ghosts_below_here():
        for copy in ghost_copies(False):
            copy.wait_recv()

    each_side(ghosts_below_here, ghosts_here)

    def before(f):
        return jnp.where(lane == 0, 0.0, pltpu.roll(f, 1, 1))

    def after(f):
        return jnp.where(lane == depth - 1, 0.0, pltpu.roll(f, depth - 1, 1))

    def here(c, i):
        return S[c, i, TOP : TOP + width]

    def south(c, i):
        return S[c, i, TOP - 1 : TOP - 1 + width]

    def new_vel(i, t):
        if i == 0:
            west = [up_in[t, c] for c in range(3)]
        else:
            west = [here(c, i - 1) for c in CROSS]
        sxx, syy, szz, sxy, sxz, syz = (here(c, i) for c in range(6))
        b = M[2, i]
        ax = (sxx - west[0]) + (sxy - south(3, i)) + (sxz - before(sxz)) + E[t, 0, i]
        ay = (sxy - west[1]) + (syy - south(1, i)) + (syz - before(syz)) + E[t, 1, i]
        az = (sxz - west[2]) + (syz - south(5, i)) + (szz - before(szz)) + E[t, 2, i]
        return [V[c, i, :width] + b * a for c, a in enumerate((ax, ay, az))]

    def new_sig(i, t):
        vx, vy, vz = (V[c, i, :width] for c in range(3))
        nx, ny, nz = (V[c, i, 1 : 1 + width] for c in range(3))
        if i == n - 1:
            ex, ey, ez = (down_in[t, c] for c in range(3))
        else:
            ex, ey, ez = (V[c, i + 1, :width] for c in range(3))
        lam, mu = M[0, i], M[1, i]
        mu2 = mu + mu
        xx, yy, zz = ex - vx, ny - vy, after(vz) - vz
        zz_in = E[t, 5, i]
        spread_all = lam * (xx + yy + zz)
        return [
            here(0, i) + (spread_all + mu2 * xx),
            here(1, i) + (spread_all + mu2 * yy),
            here(2, i) + (spread_all + mu2 * zz + (lam + mu2) * zz_in),
            here(3, i) + mu * ((nx - vx) + (ey - vy)),
            here(4, i) + mu * ((after(vx) - vx) + (ez - vz) + E[t, 3, i]),
            here(5, i) + mu * ((after(vy) - vy) + (nz - vz) + E[t, 4, i]),
        ]

    def set_vel(i, t):
        values = new_vel(i, t)
        for c in range(3):
            V[c, i, :width] = values[c]
        return values

    def set_sig(i, t):
        values = new_sig(i, t)
        for c in range(6):
            S[c, i, TOP : TOP + width] = values[c]
        return values

    def down_copy(t):
        return pltpu.make_async_remote_copy(
            src_ref=down_out.at[t],
            dst_ref=down_in.at[t],
            send_sem=down_send.at[t],
            recv_sem=down_recv.at[t],
            device_id=(group, lower),
            device_id_type=MESH,
        )

    def up_copy(t):
        return pltpu.make_async_remote_copy(
            src_ref=up_out.at[t],
            dst_ref=up_in.at[t + 1],
            send_sem=up_send.at[t],
            recv_sem=up_recv.at[t],
            device_id=(group, upper),
            device_id_type=MESH,
        )

    last_up = steps - 2 - BELOW

    def finish_top(t):
        @pl.when(has_upper)
        def _():
            down_copy(t - 1).wait_recv()

        set_sig(n - 1, t - 1)

    def send_up(t):
        values = set_sig(uplane, t)

        @pl.when(jnp.logical_and(has_upper, t <= last_up))
        def _():
            for at, c in enumerate(CROSS):
                up_out[t, at] = values[c]
            up_copy(t).start()

    def one_step(t, carry):
        values = set_vel(dplane, t)

        @pl.when(has_lower)
        def _():
            for c in range(3):
                down_out[t, c] = values[c]
            down_copy(t).start()

        done = [dplane]
        early = uplane + 1 <= n - 2
        if early:
            for i in (uplane, uplane + 1):
                if i not in done and i > 0:
                    set_vel(i, t)
                    done.append(i)
            send_up(t)
        for i in range(1, n - 1):
            if i not in done:
                set_vel(i, t)

        @pl.when(t > 0)
        def _():
            finish_top(t)

        set_vel(n - 1, t)
        if not early:
            send_up(t)
        for i in range(n - 2, 0, -1):
            if i != uplane:
                set_sig(i, t)

        @pl.when(jnp.logical_and(has_lower, t > 0))
        def _():
            up_copy(t - 1).wait_recv()

        set_vel(0, t)
        set_sig(0, t)
        return carry

    lax.fori_loop(0, steps - 1, one_step, 0)

    t = steps - 1

    out_copies = []

    def store(ref, out, i, values, kind):
        x = i - own
        for c, value in enumerate(values):
            ref[c, x] = value
        copy = pltpu.make_async_copy(ref.at[:, x], out.at[0, :, x], out_sem.at[kind, x])
        copy.start()
        out_copies.append(copy)

    if BELOW == 0:

        @pl.when(has_lower)
        def _():
            up_copy(t - 1).wait_recv()

    for i in range(own, own + planes):
        values = set_vel(i, t)
        store(vel_last, vel_out, i, values, 0)
    for i in range(own, own + planes - 1):
        store(sig_last, sig_out, i, new_sig(i, t), 1)
    finish_top(t)
    set_vel(own + planes, t)
    i = own + planes - 1
    store(sig_last, sig_out, i, new_sig(i, t), 1)

    for k in level_slots(1):
        block_copy(1, group, (lax.rem(group + k, groups), slab), k).wait_send()

    def sent_low():
        for k in level_slots(2):
            block_copy(2, group, (lax.rem(group + k, groups), lower), k).wait_send()
        for copy in ghost_copies(True):
            copy.wait_send()
        for s in range(steps - 1):
            down_copy(s).wait_send()

    def sent_high():
        for k in level_slots(0):
            block_copy(0, group, (lax.rem(group + k, groups), upper), k).wait_send()
        for copy in ghost_copies(False):
            copy.wait_send()
        for s in range(last_up + 1):
            up_copy(s).wait_send()

    each_side(sent_low, sent_high)
    for copy in out_copies:
        copy.wait()


def hand_over(vel_ref, sig_ref, vel_out, sig_out, vel_here, sig_here, load_sem, store_sem):
    pairs = [(vel_ref, vel_here, vel_out, c) for c in range(3)]
    pairs += [(sig_ref, sig_here, sig_out, c) for c in range(6)]
    loads = [
        pltpu.make_async_copy(src.at[0, c], held.at[c], load_sem.at[at])
        for at, (src, held, dst, c) in enumerate(pairs)
    ]
    stores = [
        pltpu.make_async_copy(held.at[c], dst.at[0, c], store_sem.at[at])
        for at, (src, held, dst, c) in enumerate(pairs)
    ]
    for load in loads:
        load.start()
    for load, store in zip(loads, stores):
        load.wait()
        store.start()
    for store in stores:
        store.wait()


def body(
    groups,
    slabs,
    velocity,
    stress,
    lame_lambda,
    shear_modulus,
    buoyancy,
    surface,
    block_owner,
    candidates,
    candidate_of_group,
):
    planes, width, depth = velocity.shape[1:]
    steps, parts = surface.shape[:2]
    columns = surface.shape[3]
    n = BELOW + planes + ABOVE
    lanes = steps * CHUNK
    far = pl.BlockSpec(memory_space=pl.ANY)
    scalars = pl.BlockSpec(memory_space=pltpu.SMEM)
    f32 = jnp.float32
    message = pltpu.VMEM((steps, 3, width, depth), f32)
    dma = pltpu.SemaphoreType.DMA
    shapes = (
        jax.ShapeDtypeStruct((1, 3, planes, width, depth), f32),
        jax.ShapeDtypeStruct((1, 6, planes, width, depth), f32),
    )
    vel, sig = pl.pallas_call(
        functools.partial(kernel, groups, slabs, steps),
        out_shape=shapes,
        in_specs=[scalars] * 3 + [far] * 6,
        out_specs=(far, far),
        scratch_shapes=[
            pltpu.VMEM((3, n, width + 8, depth), f32),
            pltpu.VMEM((6, n, width + TOP, depth), f32),
            pltpu.VMEM((3, n, width, depth), f32),
            pltpu.VMEM((steps, 6, n, width, depth), f32),
            pltpu.VMEM((3, planes, width, depth), jnp.bfloat16),
            pltpu.VMEM((steps * parts, planes, columns), f32),
            pltpu.VMEM((lanes, 128), f32),
            pltpu.VMEM((columns, lanes), f32),
            pltpu.VMEM((3, groups, columns, lanes), f32),
            pltpu.VMEM((3, width, lanes), f32),
            pltpu.VMEM((steps, 3, width, 128), f32),
            message,
            message,
            message,
            message,
            pltpu.VMEM((3, planes, width, depth), f32),
            pltpu.VMEM((6, planes, width, depth), f32),
            dma((6,)),
            dma((3, groups)),
            dma((3, groups)),
            dma((8,)),
            dma((8,)),
            dma((steps,)),
            dma((steps,)),
            dma((steps,)),
            dma((steps,)),
            dma((2, planes)),
        ],
        compiler_params=pltpu.CompilerParams(
            collective_id=0, has_side_effects=True, vmem_limit_bytes=VMEM
        ),
    )(
        block_owner,
        candidates.T,
        candidate_of_group,
        velocity,
        stress,
        lame_lambda,
        shear_modulus,
        buoyancy,
        surface.reshape(steps * parts, planes, columns),
    )
    return pl.pallas_call(
        hand_over,
        out_shape=shapes,
        in_specs=[far, far],
        out_specs=(far, far),
        scratch_shapes=[
            pltpu.VMEM((3, planes, width, depth), f32),
            pltpu.VMEM((6, planes, width, depth), f32),
            dma((9,)),
            dma((9,)),
        ],
        compiler_params=pltpu.CompilerParams(vmem_limit_bytes=VMEM),
    )(vel, sig)


def solution(mesh):
    in_specs = (
        P(None, "slab", None, None),
        P(None, "slab", None, None),
        P("slab", None, None),
        P("slab", None, None),
        P("slab", None, None),
        P(None, None, "slab", "cand"),
        P(),
        P(),
        P(),
    )
    out_specs = (P("cand", None, "slab", None, None), P("cand", None, "slab", None, None))
    return jax.shard_map(
        functools.partial(body, mesh.shape["cand"], mesh.shape["slab"]),
        mesh=mesh,
        in_specs=in_specs,
        out_specs=out_specs,
        check_vma=False,
    )
```

```python
import functools

import jax
import jax.numpy as jnp
from jax import lax
from jax.experimental import pallas as pl
from jax.experimental.pallas import tpu as pltpu
from jax.sharding import PartitionSpec as P

DT = 0.15
VMEM = 62 * 1024 * 1024
MESH = pl.DeviceIdType.MESH
ABOVE = 1
BELOW = 1
TOP = 8
CHUNK = 32
CROSS = (0, 3, 4)


def kernel(
    groups,
    slabs,
    steps,
    owner_ref,
    table_ref,
    order_ref,
    vel_ref,
    sig_ref,
    lam_ref,
    mu_ref,
    buoy_ref,
    surface_ref,
    vel_out,
    sig_out,
    V,
    S,
    M,
    raw,
    raw_rows,
    tall,
    packed,
    blocks_low,
    blocks_own,
    blocks_high,
    rows,
    per_step,
    down_in,
    up_in,
    down_out,
    up_out,
    vel_last,
    sig_last,
    local_sem,
    block_send,
    block_recv,
    ghost_send,
    ghost_recv,
    down_send,
    down_recv,
    up_send,
    up_recv,
    out_sem,
):
    blocks = (blocks_low, blocks_own, blocks_high)
    planes, width, depth = vel_ref.shape[1:]
    n = BELOW + planes + ABOVE
    own = BELOW
    group = lax.axis_index("cand")
    slab = lax.axis_index("slab")
    has_lower = slab > 0
    has_upper = slab < slabs - 1
    lower, upper = slab - 1, slab + 1
    dplane = own + ABOVE
    uplane = own + planes - 1 - BELOW

    barrier = pltpu.get_barrier_semaphore()
    for k in range(1, groups):
        pl.semaphore_signal(
            barrier, inc=1, device_id=(lax.rem(group + k, groups), slab), device_id_type=MESH
        )

    @pl.when(has_lower)
    def _():
        for k in range(groups):
            pl.semaphore_signal(
                barrier, inc=1, device_id=(lax.rem(group + k, groups), lower), device_id_type=MESH
            )

    @pl.when(has_upper)
    def _():
        for k in range(groups):
            pl.semaphore_signal(
                barrier, inc=1, device_id=(lax.rem(group + k, groups), upper), device_id_type=MESH
            )

    parts = surface_ref.shape[0] // steps
    columns = width // groups
    loads = [
        pltpu.make_async_copy(lam_ref, raw.at[0], local_sem.at[0]),
        pltpu.make_async_copy(mu_ref, raw.at[1], local_sem.at[1]),
        pltpu.make_async_copy(buoy_ref, raw.at[2], local_sem.at[2]),
        pltpu.make_async_copy(surface_ref, raw_rows, local_sem.at[3]),
        pltpu.make_async_copy(
            vel_ref, V.at[:, pl.ds(own, planes), pl.ds(0, width)], local_sem.at[4]
        ),
        pltpu.make_async_copy(
            sig_ref, S.at[:, pl.ds(own, planes), pl.ds(TOP, width)], local_sem.at[5]
        ),
    ]
    for load in loads:
        load.start()

    V[:, :, width:] = jnp.zeros((3, n, V.shape[2] - width, depth), jnp.float32)
    S[:, :, :TOP] = jnp.zeros((6, n, TOP, depth), jnp.float32)

    @pl.when(jnp.logical_not(has_lower))
    def _():
        up_in[...] = jnp.zeros_like(up_in)
        blocks_low[...] = jnp.zeros_like(blocks_low)
        if BELOW:
            V[:, :BELOW, :width] = jnp.zeros((3, BELOW, width, depth), jnp.float32)
            S[:, :BELOW, TOP:] = jnp.zeros((6, BELOW, width, depth), jnp.float32)
            M[:, :BELOW] = jnp.zeros((3, BELOW, width, depth), jnp.float32)

    @pl.when(jnp.logical_not(has_upper))
    def _():
        down_in[...] = jnp.zeros_like(down_in)
        blocks_high[...] = jnp.zeros_like(blocks_high)
        if ABOVE:
            V[:, n - ABOVE :, :width] = jnp.zeros((3, ABOVE, width, depth), jnp.float32)
            S[:, n - ABOVE :, TOP:] = jnp.zeros((6, ABOVE, width, depth), jnp.float32)
            M[:, n - ABOVE :] = jnp.zeros((3, ABOVE, width, depth), jnp.float32)

    tall[...] = jnp.zeros_like(tall)
    loads[3].wait()
    for t in range(steps):
        for c in range(parts):
            at = t * CHUNK + c * planes
            tall[at : at + planes, :columns] = raw_rows[t * parts + c]
    for at in range(0, steps * CHUNK, 128):
        turned = tall[at : at + 128, :].T[:columns]
        packed[:, at : at + 128] = turned
        blocks_own[group, :, at : at + 128] = turned

    lane = lax.broadcasted_iota(jnp.int32, (width, depth), 1)
    zone = lax.broadcasted_iota(jnp.int32, (planes, width, depth), 2) >= depth // 2
    chosen = order_ref[group]
    for load in loads[:3]:
        load.wait()
    for which in range(3):
        scale = jnp.where(zone, table_ref[which, chosen] * DT, DT)
        M[which, own : own + planes] = raw[which].astype(jnp.float32) * scale

    sides = has_lower.astype(jnp.int32) + has_upper.astype(jnp.int32)
    pl.semaphore_wait(barrier, groups - 1 + groups * sides)

    def block_copy(level, slot, to, index):
        return pltpu.make_async_remote_copy(
            src_ref=packed,
            dst_ref=blocks[level].at[slot],
            send_sem=block_send.at[level, index],
            recv_sem=block_recv.at[level, slot],
            device_id=to,
            device_id_type=MESH,
        )

    def ghost_copies(down):
        count, to = (ABOVE, lower) if down else (BELOW, upper)
        base = 0 if down else 3
        source = 0 if down else planes - BELOW
        target = own + planes if down else 0
        pairs = []
        if count:
            there = pl.ds(target, count)
            pairs = [
                (sig_ref.at[:, pl.ds(source, count)], S.at[:, there, pl.ds(TOP, width)]),
                (vel_ref.at[:, pl.ds(source, count)], V.at[:, there, pl.ds(0, width)]),
                (M.at[:, pl.ds(own + source, count)], M.at[:, there]),
            ]
        else:
            base = 3
        if not down:
            edge = planes - 1 - BELOW
            pairs.append((sig_ref.at[0, edge], up_in.at[0, 0]))
            pairs.append((sig_ref.at[pl.ds(3, 2), edge], up_in.at[0, pl.ds(1, 2)]))
        return [
            pltpu.make_async_remote_copy(
                src_ref=src,
                dst_ref=dst,
                send_sem=ghost_send.at[base + at],
                recv_sem=ghost_recv.at[base + at],
                device_id=(group, to),
                device_id_type=MESH,
            )
            for at, (src, dst) in enumerate(pairs)
        ]

    def level_slots(level):
        return range(1 if level == 1 else 0, groups)

    def send_blocks(level, to):
        for k in level_slots(level):
            block_copy(level, group, (lax.rem(group + k, groups), to), k).start()

    def each_side(low, high):
        pl.when(has_lower)(low)
        pl.when(has_upper)(high)

    send_blocks(1, slab)

    def first_low():
        send_blocks(2, lower)
        for copy in ghost_copies(True):
            copy.start()

    def first_high():
        send_blocks(0, upper)
        for copy in ghost_copies(False):
            copy.start()

    each_side(first_low, first_high)

    def take_blocks(level, to):
        for k in level_slots(level):
            slot = lax.rem(group + k, groups)
            block_copy(level, slot, (slot, to), k).wait_recv()

    halves = 128 // CHUNK

    def prepare(level):
        for j in range(groups):
            rows[level, j * columns : (j + 1) * columns] = blocks[level][owner_ref[j]]
        for t in range(steps):
            at = 128 * (t // halves)
            piece = rows[level, :, at : at + 128]
            shift = (t % halves) * CHUNK
            per_step[t, level] = pltpu.roll(piece, 128 - shift, 1) if shift else piece

    take_blocks(1, slab)
    prepare(1)
    source_level = depth // 8

    def pulse(t, c, i):
        x = i - own
        level = 0 if x < 0 else 2 if x >= planes else 1
        at = c * planes + x % planes
        moved = pltpu.roll(per_step[t, level], (source_level - at) % depth, 1)
        return jnp.where(lane == source_level, moved, 0.0)

    for load in loads[4:]:
        load.wait()

    def arrive_top():
        @pl.when(has_upper)
        def _():
            for copy in ghost_copies(True):
                copy.wait_recv()
            take_blocks(2, upper)

        prepare(2)

    def arrive_bottom():
        @pl.when(has_lower)
        def _():
            for copy in ghost_copies(False):
                copy.wait_recv()
            take_blocks(0, lower)

        prepare(0)

    def before(f):
        return jnp.where(lane == 0, 0.0, pltpu.roll(f, 1, 1))

    def after(f):
        return jnp.where(lane == depth - 1, 0.0, pltpu.roll(f, depth - 1, 1))

    def here(c, i):
        return S[c, i, TOP : TOP + width]

    def south(c, i):
        return S[c, i, TOP - 1 : TOP - 1 + width]

    def new_vel(i, t):
        if i == 0:
            west = [up_in[t, c] for c in range(3)]
        else:
            west = [here(c, i - 1) for c in CROSS]
        sxx, syy, szz, sxy, sxz, syz = (here(c, i) for c in range(6))
        b = M[2, i]
        ax = (sxx - west[0]) + (sxy - south(3, i)) + (sxz - before(sxz)) + pulse(t, 0, i)
        ay = (sxy - west[1]) + (syy - south(1, i)) + (syz - before(syz)) + pulse(t, 1, i)
        az = (sxz - west[2]) + (syz - south(5, i)) + (szz - before(szz)) + pulse(t, 2, i)
        return [V[c, i, :width] + b * a for c, a in enumerate((ax, ay, az))]

    def new_sig(i, t):
        vx, vy, vz = (V[c, i, :width] for c in range(3))
        nx, ny, nz = (V[c, i, 1 : 1 + width] for c in range(3))
        if i == n - 1:
            ex, ey, ez = (down_in[t, c] for c in range(3))
        else:
            ex, ey, ez = (V[c, i + 1, :width] for c in range(3))
        lam, mu = M[0, i], M[1, i]
        mu2 = mu + mu
        xx, yy, zz = ex - vx, ny - vy, after(vz) - vz
        zz_in = pulse(t, 5, i)
        spread_all = lam * (xx + yy + zz)
        return [
            here(0, i) + (spread_all + mu2 * xx),
            here(1, i) + (spread_all + mu2 * yy),
            here(2, i) + (spread_all + mu2 * zz + (lam + mu2) * zz_in),
            here(3, i) + mu * ((nx - vx) + (ey - vy)),
            here(4, i) + mu * ((after(vx) - vx) + (ez - vz) + pulse(t, 3, i)),
            here(5, i) + mu * ((after(vy) - vy) + (nz - vz) + pulse(t, 4, i)),
        ]

    def set_vel(i, t):
        values = new_vel(i, t)
        for c in range(3):
            V[c, i, :width] = values[c]
        return values

    def set_sig(i, t):
        values = new_sig(i, t)
        for c in range(6):
            S[c, i, TOP : TOP + width] = values[c]
        return values

    def down_copy(t):
        return pltpu.make_async_remote_copy(
            src_ref=down_out.at[t],
            dst_ref=down_in.at[t],
            send_sem=down_send.at[t],
            recv_sem=down_recv.at[t],
            device_id=(group, lower),
            device_id_type=MESH,
        )

    def up_copy(t):
        return pltpu.make_async_remote_copy(
            src_ref=up_out.at[t],
            dst_ref=up_in.at[t + 1],
            send_sem=up_send.at[t],
            recv_sem=up_recv.at[t],
            device_id=(group, upper),
            device_id_type=MESH,
        )

    last_up = steps - 2 - BELOW

    def finish_top(t):
        @pl.when(has_upper)
        def _():
            down_copy(t - 1).wait_recv()

        set_sig(n - 1, t - 1)

    def send_up(t):
        values = set_sig(uplane, t)

        @pl.when(jnp.logical_and(has_upper, t <= last_up))
        def _():
            for at, c in enumerate(CROSS):
                up_out[t, at] = values[c]
            up_copy(t).start()

    def one_step(t, carry):
        values = set_vel(dplane, t)

        @pl.when(has_lower)
        def _():
            for c in range(3):
                down_out[t, c] = values[c]
            down_copy(t).start()

        done = [dplane]
        early = uplane + 1 <= n - 2
        if early:
            for i in (uplane, uplane + 1):
                if i not in done and i > 0:
                    set_vel(i, t)
                    done.append(i)
            send_up(t)
        for i in range(own + 1, own + planes):
            if i not in done:
                set_vel(i, t)

        pl.when(t == 0)(arrive_top)

        @pl.when(t > 0)
        def _():
            finish_top(t)

        for i in range(own + planes, n):
            set_vel(i, t)
        if not early:
            send_up(t)
        for i in range(n - 2, own, -1):
            if i != uplane:
                set_sig(i, t)

        @pl.when(jnp.logical_and(has_lower, t > 0))
        def _():
            up_copy(t - 1).wait_recv()

        pl.when(t == 0)(arrive_bottom)
        for i in range(own, -1, -1):
            set_vel(i, t)
        for i in range(own, -1, -1):
            set_sig(i, t)
        return carry

    lax.fori_loop(0, steps - 1, one_step, 0)

    t = steps - 1

    out_copies = []

    def store(ref, out, i, values, kind):
        x = i - own
        for c, value in enumerate(values):
            ref[c, x] = value
        copy = pltpu.make_async_copy(ref.at[:, x], out.at[0, :, x], out_sem.at[kind, x])
        copy.start()
        out_copies.append(copy)

    if BELOW == 0:

        @pl.when(has_lower)
        def _():
            up_copy(t - 1).wait_recv()

    for i in range(own, own + planes):
        values = set_vel(i, t)
        store(vel_last, vel_out, i, values, 0)
    for i in range(own, own + planes - 1):
        store(sig_last, sig_out, i, new_sig(i, t), 1)
    finish_top(t)
    set_vel(own + planes, t)
    i = own + planes - 1
    store(sig_last, sig_out, i, new_sig(i, t), 1)

    for k in level_slots(1):
        block_copy(1, group, (lax.rem(group + k, groups), slab), k).wait_send()

    def sent_low():
        for k in level_slots(2):
            block_copy(2, group, (lax.rem(group + k, groups), lower), k).wait_send()
        for copy in ghost_copies(True):
            copy.wait_send()
        for s in range(steps - 1):
            down_copy(s).wait_send()

    def sent_high():
        for k in level_slots(0):
            block_copy(0, group, (lax.rem(group + k, groups), upper), k).wait_send()
        for copy in ghost_copies(False):
            copy.wait_send()
        for s in range(last_up + 1):
            up_copy(s).wait_send()

    each_side(sent_low, sent_high)
    for copy in out_copies:
        copy.wait()


def hand_over(vel_ref, sig_ref, vel_out, sig_out, vel_here, sig_here, load_sem, store_sem):
    pairs = [(vel_ref, vel_here, vel_out, c) for c in range(3)]
    pairs += [(sig_ref, sig_here, sig_out, c) for c in range(6)]
    loads = [
        pltpu.make_async_copy(src.at[0, c], held.at[c], load_sem.at[at])
        for at, (src, held, dst, c) in enumerate(pairs)
    ]
    stores = [
        pltpu.make_async_copy(held.at[c], dst.at[0, c], store_sem.at[at])
        for at, (src, held, dst, c) in enumerate(pairs)
    ]
    for load in loads:
        load.start()
    for load, store in zip(loads, stores):
        load.wait()
        store.start()
    for store in stores:
        store.wait()


def body(
    groups,
    slabs,
    velocity,
    stress,
    lame_lambda,
    shear_modulus,
    buoyancy,
    surface,
    block_owner,
    candidates,
    candidate_of_group,
):
    planes, width, depth = velocity.shape[1:]
    steps, parts = surface.shape[:2]
    columns = surface.shape[3]
    n = BELOW + planes + ABOVE
    lanes = steps * CHUNK
    far = pl.BlockSpec(memory_space=pl.ANY)
    scalars = pl.BlockSpec(memory_space=pltpu.SMEM)
    f32 = jnp.float32
    message = pltpu.VMEM((steps, 3, width, depth), f32)
    dma = pltpu.SemaphoreType.DMA
    shapes = (
        jax.ShapeDtypeStruct((1, 3, planes, width, depth), f32),
        jax.ShapeDtypeStruct((1, 6, planes, width, depth), f32),
    )
    vel, sig = pl.pallas_call(
        functools.partial(kernel, groups, slabs, steps),
        out_shape=shapes,
        in_specs=[scalars] * 3 + [far] * 6,
        out_specs=(far, far),
        scratch_shapes=[
            pltpu.VMEM((3, n, width + 8, depth), f32),
            pltpu.VMEM((6, n, width + TOP, depth), f32),
            pltpu.VMEM((3, n, width, depth), f32),
            pltpu.VMEM((3, planes, width, depth), jnp.bfloat16),
            pltpu.VMEM((steps * parts, planes, columns), f32),
            pltpu.VMEM((lanes, 128), f32),
            pltpu.VMEM((columns, lanes), f32),
            pltpu.VMEM((groups, columns, lanes), f32),
            pltpu.VMEM((groups, columns, lanes), f32),
            pltpu.VMEM((groups, columns, lanes), f32),
            pltpu.VMEM((3, width, lanes), f32),
            pltpu.VMEM((steps, 3, width, 128), f32),
            message,
            message,
            message,
            message,
            pltpu.VMEM((3, planes, width, depth), f32),
            pltpu.VMEM((6, planes, width, depth), f32),
            dma((6,)),
            dma((3, groups)),
            dma((3, groups)),
            dma((8,)),
            dma((8,)),
            dma((steps,)),
            dma((steps,)),
            dma((steps,)),
            dma((steps,)),
            dma((2, planes)),
        ],
        compiler_params=pltpu.CompilerParams(
            collective_id=0, has_side_effects=True, vmem_limit_bytes=VMEM
        ),
    )(
        block_owner,
        candidates.T,
        candidate_of_group,
        velocity,
        stress,
        lame_lambda,
        shear_modulus,
        buoyancy,
        surface.reshape(steps * parts, planes, columns),
    )
    return pl.pallas_call(
        hand_over,
        out_shape=shapes,
        in_specs=[far, far],
        out_specs=(far, far),
        scratch_shapes=[
            pltpu.VMEM((3, planes, width, depth), f32),
            pltpu.VMEM((6, planes, width, depth), f32),
            dma((9,)),
            dma((9,)),
        ],
        compiler_params=pltpu.CompilerParams(vmem_limit_bytes=VMEM),
    )(vel, sig)


def solution(mesh):
    in_specs = (
        P(None, "slab", None, None),
        P(None, "slab", None, None),
        P("slab", None, None),
        P("slab", None, None),
        P("slab", None, None),
        P(None, None, "slab", "cand"),
        P(),
        P(),
        P(),
    )
    out_specs = (P("cand", None, "slab", None, None), P("cand", None, "slab", None, None))
    return jax.shard_map(
        functools.partial(body, mesh.shape["cand"], mesh.shape["slab"]),
        mesh=mesh,
        in_specs=in_specs,
        out_specs=out_specs,
        check_vma=False,
    )
```

```python
import functools

import jax
import jax.numpy as jnp
from jax import lax
from jax.experimental import pallas as pl
from jax.experimental.pallas import tpu as pltpu
from jax.sharding import PartitionSpec as P

DT = 0.15
VMEM = 62 * 1024 * 1024
MESH = pl.DeviceIdType.MESH
ABOVE = 1
BELOW = 1
TOP = 8
CHUNK = 32
CROSS = (0, 3, 4)


def kernel(
    groups,
    slabs,
    steps,
    owner_ref,
    table_ref,
    order_ref,
    vel_ref,
    sig_ref,
    lam_ref,
    mu_ref,
    buoy_ref,
    surface_ref,
    vel_out,
    sig_out,
    V,
    S,
    M,
    raw,
    raw_rows,
    tall,
    packed,
    blocks_low,
    blocks_own,
    blocks_high,
    rows,
    per_step,
    down_in,
    up_in,
    down_out,
    up_out,
    first_out,
    vel_last,
    sig_last,
    local_sem,
    block_send,
    block_recv,
    ghost_send,
    ghost_recv,
    down_send,
    down_recv,
    up_send,
    up_recv,
    out_sem,
):
    blocks = (blocks_low, blocks_own, blocks_high)
    planes, width, depth = vel_ref.shape[1:]
    n = BELOW + planes + ABOVE
    own = BELOW
    group = lax.axis_index("cand")
    slab = lax.axis_index("slab")
    has_lower = slab > 0
    has_upper = slab < slabs - 1
    lower, upper = slab - 1, slab + 1
    dplane = own + ABOVE
    uplane = own + planes - 1 - BELOW

    barrier = pltpu.get_barrier_semaphore()
    for k in range(1, groups):
        pl.semaphore_signal(
            barrier, inc=1, device_id=(lax.rem(group + k, groups), slab), device_id_type=MESH
        )

    @pl.when(has_lower)
    def _():
        for k in range(groups):
            pl.semaphore_signal(
                barrier, inc=1, device_id=(lax.rem(group + k, groups), lower), device_id_type=MESH
            )

    @pl.when(has_upper)
    def _():
        for k in range(groups):
            pl.semaphore_signal(
                barrier, inc=1, device_id=(lax.rem(group + k, groups), upper), device_id_type=MESH
            )

    parts = surface_ref.shape[0] // steps
    columns = width // groups
    loads = [
        pltpu.make_async_copy(lam_ref, raw.at[0], local_sem.at[0]),
        pltpu.make_async_copy(mu_ref, raw.at[1], local_sem.at[1]),
        pltpu.make_async_copy(buoy_ref, raw.at[2], local_sem.at[2]),
        pltpu.make_async_copy(surface_ref, raw_rows, local_sem.at[3]),
        pltpu.make_async_copy(
            vel_ref, V.at[:, pl.ds(own, planes), pl.ds(0, width)], local_sem.at[4]
        ),
        pltpu.make_async_copy(
            sig_ref, S.at[:, pl.ds(own, planes), pl.ds(TOP, width)], local_sem.at[5]
        ),
    ]
    for load in loads:
        load.start()

    V[:, :, width:] = jnp.zeros((3, n, V.shape[2] - width, depth), jnp.float32)
    S[:, :, :TOP] = jnp.zeros((6, n, TOP, depth), jnp.float32)

    @pl.when(jnp.logical_not(has_lower))
    def _():
        up_in[...] = jnp.zeros_like(up_in)
        blocks_low[...] = jnp.zeros_like(blocks_low)
        if BELOW:
            V[:, :BELOW, :width] = jnp.zeros((3, BELOW, width, depth), jnp.float32)
            S[:, :BELOW, TOP:] = jnp.zeros((6, BELOW, width, depth), jnp.float32)
            M[:, :BELOW] = jnp.zeros((3, BELOW, width, depth), jnp.float32)

    @pl.when(jnp.logical_not(has_upper))
    def _():
        down_in[...] = jnp.zeros_like(down_in)
        blocks_high[...] = jnp.zeros_like(blocks_high)
        if ABOVE:
            V[:, n - ABOVE :, :width] = jnp.zeros((3, ABOVE, width, depth), jnp.float32)
            S[:, n - ABOVE :, TOP:] = jnp.zeros((6, ABOVE, width, depth), jnp.float32)
            M[:, n - ABOVE :] = jnp.zeros((3, ABOVE, width, depth), jnp.float32)

    tall[...] = jnp.zeros_like(tall)
    loads[3].wait()
    for t in range(steps):
        for c in range(parts):
            at = t * CHUNK + c * planes
            tall[at : at + planes, :columns] = raw_rows[t * parts + c]
    for at in range(0, steps * CHUNK, 128):
        turned = tall[at : at + 128, :].T[:columns]
        packed[:, at : at + 128] = turned
        blocks_own[group, :, at : at + 128] = turned

    lane = lax.broadcasted_iota(jnp.int32, (width, depth), 1)
    zone = lax.broadcasted_iota(jnp.int32, (planes, width, depth), 2) >= depth // 2
    chosen = order_ref[group]
    for load in loads[:3]:
        load.wait()
    for which in range(3):
        scale = jnp.where(zone, table_ref[which, chosen] * DT, DT)
        M[which, own : own + planes] = raw[which].astype(jnp.float32) * scale

    sides = has_lower.astype(jnp.int32) + has_upper.astype(jnp.int32)
    pl.semaphore_wait(barrier, groups - 1 + groups * sides)

    def block_copy(level, slot, to, index):
        return pltpu.make_async_remote_copy(
            src_ref=packed,
            dst_ref=blocks[level].at[slot],
            send_sem=block_send.at[level, index],
            recv_sem=block_recv.at[level, slot],
            device_id=to,
            device_id_type=MESH,
        )

    def ghost_copies(down):
        to = lower if down else upper
        base = 0 if down else 3
        edge = 0 if down else planes - 1
        there = n - 1 if down else 0
        pairs = [
            (sig_ref.at[:, edge], S.at[:, there, pl.ds(TOP, width)]),
            (M.at[:, own + edge], M.at[:, there]),
        ]
        if down:
            pairs.append((vel_ref.at[:, edge], V.at[:, there, pl.ds(0, width)]))
        return [
            pltpu.make_async_remote_copy(
                src_ref=src,
                dst_ref=dst,
                send_sem=ghost_send.at[base + at],
                recv_sem=ghost_recv.at[base + at],
                device_id=(group, to),
                device_id_type=MESH,
            )
            for at, (src, dst) in enumerate(pairs)
        ]

    def first_copy():
        return pltpu.make_async_remote_copy(
            src_ref=first_out,
            dst_ref=V.at[:, 0, pl.ds(0, width)],
            send_sem=ghost_send.at[5],
            recv_sem=ghost_recv.at[5],
            device_id=(group, upper),
            device_id_type=MESH,
        )

    def level_slots(level):
        return range(1 if level == 1 else 0, groups)

    def send_blocks(level, to):
        for k in level_slots(level):
            block_copy(level, group, (lax.rem(group + k, groups), to), k).start()

    def each_side(low, high):
        pl.when(has_lower)(low)
        pl.when(has_upper)(high)

    send_blocks(1, slab)

    def first_low():
        send_blocks(2, lower)
        for copy in ghost_copies(True):
            copy.start()

    def first_high():
        send_blocks(0, upper)
        for copy in ghost_copies(False):
            copy.start()

    each_side(first_low, first_high)

    def take_blocks(level, to):
        for k in level_slots(level):
            slot = lax.rem(group + k, groups)
            block_copy(level, slot, (slot, to), k).wait_recv()

    halves = 128 // CHUNK

    def prepare(level):
        for j in range(groups):
            rows[level, j * columns : (j + 1) * columns] = blocks[level][owner_ref[j]]
        for t in range(steps):
            at = 128 * (t // halves)
            piece = rows[level, :, at : at + 128]
            shift = (t % halves) * CHUNK
            per_step[t, level] = pltpu.roll(piece, 128 - shift, 1) if shift else piece

    take_blocks(1, slab)
    prepare(1)
    source_level = depth // 8

    def pulse(t, c, i):
        x = i - own
        level = 0 if x < 0 else 2 if x >= planes else 1
        at = c * planes + x % planes
        moved = pltpu.roll(per_step[t, level], (source_level - at) % depth, 1)
        return jnp.where(lane == source_level, moved, 0.0)

    for load in loads[4:]:
        load.wait()

    def arrive_top():
        @pl.when(has_upper)
        def _():
            for copy in ghost_copies(True):
                copy.wait_recv()
            take_blocks(2, upper)

        prepare(2)

    def arrive_bottom():
        @pl.when(has_lower)
        def _():
            for copy in ghost_copies(False):
                copy.wait_recv()
            take_blocks(0, lower)
            first_copy().wait_recv()

        prepare(0)

    def before(f):
        return jnp.where(lane == 0, 0.0, pltpu.roll(f, 1, 1))

    def after(f):
        return jnp.where(lane == depth - 1, 0.0, pltpu.roll(f, depth - 1, 1))

    def here(c, i):
        return S[c, i, TOP : TOP + width]

    def south(c, i):
        return S[c, i, TOP - 1 : TOP - 1 + width]

    def new_vel(i, t):
        if i == 0:
            west = [up_in[t, c] for c in range(3)]
        else:
            west = [here(c, i - 1) for c in CROSS]
        sxx, syy, szz, sxy, sxz, syz = (here(c, i) for c in range(6))
        b = M[2, i]
        ax = (sxx - west[0]) + (sxy - south(3, i)) + (sxz - before(sxz)) + pulse(t, 0, i)
        ay = (sxy - west[1]) + (syy - south(1, i)) + (syz - before(syz)) + pulse(t, 1, i)
        az = (sxz - west[2]) + (syz - south(5, i)) + (szz - before(szz)) + pulse(t, 2, i)
        return [V[c, i, :width] + b * a for c, a in enumerate((ax, ay, az))]

    def new_sig(i, t):
        vx, vy, vz = (V[c, i, :width] for c in range(3))
        nx, ny, nz = (V[c, i, 1 : 1 + width] for c in range(3))
        if i == n - 1:
            ex, ey, ez = (down_in[t, c] for c in range(3))
        else:
            ex, ey, ez = (V[c, i + 1, :width] for c in range(3))
        lam, mu = M[0, i], M[1, i]
        mu2 = mu + mu
        xx, yy, zz = ex - vx, ny - vy, after(vz) - vz
        zz_in = pulse(t, 5, i)
        spread_all = lam * (xx + yy + zz)
        return [
            here(0, i) + (spread_all + mu2 * xx),
            here(1, i) + (spread_all + mu2 * yy),
            here(2, i) + (spread_all + mu2 * zz + (lam + mu2) * zz_in),
            here(3, i) + mu * ((nx - vx) + (ey - vy)),
            here(4, i) + mu * ((after(vx) - vx) + (ez - vz) + pulse(t, 3, i)),
            here(5, i) + mu * ((after(vy) - vy) + (nz - vz) + pulse(t, 4, i)),
        ]

    def set_vel(i, t):
        values = new_vel(i, t)
        for c in range(3):
            V[c, i, :width] = values[c]
        return values

    def set_sig(i, t):
        values = new_sig(i, t)
        for c in range(6):
            S[c, i, TOP : TOP + width] = values[c]
        return values

    def down_copy(t):
        return pltpu.make_async_remote_copy(
            src_ref=down_out.at[t],
            dst_ref=down_in.at[t],
            send_sem=down_send.at[t],
            recv_sem=down_recv.at[t],
            device_id=(group, lower),
            device_id_type=MESH,
        )

    def up_copy(t):
        return pltpu.make_async_remote_copy(
            src_ref=up_out.at[t],
            dst_ref=up_in.at[t + 1],
            send_sem=up_send.at[t],
            recv_sem=up_recv.at[t],
            device_id=(group, upper),
            device_id_type=MESH,
        )

    last_up = steps - 2 - BELOW

    def finish_top(t):
        @pl.when(has_upper)
        def _():
            down_copy(t - 1).wait_recv()

        set_sig(n - 1, t - 1)

    def send_up(t):
        values = set_sig(uplane, t)

        @pl.when(jnp.logical_and(has_upper, t <= last_up))
        def _():
            for at, c in enumerate(CROSS):
                up_out[t, at] = values[c]
            up_copy(t).start()

    def one_step(t, carry):
        values = set_vel(dplane, t)

        @pl.when(has_lower)
        def _():
            for c in range(3):
                down_out[t, c] = values[c]
            down_copy(t).start()

        done = [dplane, own + planes - 1]
        values = set_vel(own + planes - 1, t)

        @pl.when(jnp.logical_and(has_upper, t == 0))
        def _():
            for c in range(3):
                first_out[c] = values[c]
            first_copy().start()

        early = uplane + 1 <= n - 2
        if early:
            for i in (uplane, uplane + 1):
                if i not in done and i > 0:
                    set_vel(i, t)
                    done.append(i)
            send_up(t)
        for i in range(own + 1, own + planes):
            if i not in done:
                set_vel(i, t)

        pl.when(t == 0)(arrive_top)

        @pl.when(t > 0)
        def _():
            finish_top(t)

        for i in range(own + planes, n):
            set_vel(i, t)
        if not early:
            send_up(t)
        for i in range(n - 2, own, -1):
            if i != uplane:
                set_sig(i, t)

        @pl.when(jnp.logical_and(has_lower, t > 0))
        def _():
            up_copy(t - 1).wait_recv()

        pl.when(t == 0)(arrive_bottom)
        set_vel(own, t)

        @pl.when(t > 0)
        def _():
            set_vel(0, t)

        for i in range(own, -1, -1):
            set_sig(i, t)
        return carry

    lax.fori_loop(0, steps - 1, one_step, 0)

    t = steps - 1

    out_copies = []

    def store(ref, out, i, values, kind):
        x = i - own
        for c, value in enumerate(values):
            ref[c, x] = value
        copy = pltpu.make_async_copy(ref.at[:, x], out.at[0, :, x], out_sem.at[kind, x])
        copy.start()
        out_copies.append(copy)

    if BELOW == 0:

        @pl.when(has_lower)
        def _():
            up_copy(t - 1).wait_recv()

    for i in range(own, own + planes):
        values = set_vel(i, t)
        store(vel_last, vel_out, i, values, 0)
    for i in range(own, own + planes - 1):
        store(sig_last, sig_out, i, new_sig(i, t), 1)
    finish_top(t)
    set_vel(own + planes, t)
    i = own + planes - 1
    store(sig_last, sig_out, i, new_sig(i, t), 1)

    for k in level_slots(1):
        block_copy(1, group, (lax.rem(group + k, groups), slab), k).wait_send()

    def sent_low():
        for k in level_slots(2):
            block_copy(2, group, (lax.rem(group + k, groups), lower), k).wait_send()
        for copy in ghost_copies(True):
            copy.wait_send()
        for s in range(steps - 1):
            down_copy(s).wait_send()

    def sent_high():
        for k in level_slots(0):
            block_copy(0, group, (lax.rem(group + k, groups), upper), k).wait_send()
        for copy in ghost_copies(False):
            copy.wait_send()
        first_copy().wait_send()
        for s in range(last_up + 1):
            up_copy(s).wait_send()

    each_side(sent_low, sent_high)
    for copy in out_copies:
        copy.wait()


def hand_over(vel_ref, sig_ref, vel_out, sig_out, vel_here, sig_here, load_sem, store_sem):
    pairs = [(vel_ref, vel_here, vel_out, c) for c in range(3)]
    pairs += [(sig_ref, sig_here, sig_out, c) for c in range(6)]
    loads = [
        pltpu.make_async_copy(src.at[0, c], held.at[c], load_sem.at[at])
        for at, (src, held, dst, c) in enumerate(pairs)
    ]
    stores = [
        pltpu.make_async_copy(held.at[c], dst.at[0, c], store_sem.at[at])
        for at, (src, held, dst, c) in enumerate(pairs)
    ]
    for load in loads:
        load.start()
    for load, store in zip(loads, stores):
        load.wait()
        store.start()
    for store in stores:
        store.wait()


def body(
    groups,
    slabs,
    velocity,
    stress,
    lame_lambda,
    shear_modulus,
    buoyancy,
    surface,
    block_owner,
    candidates,
    candidate_of_group,
):
    planes, width, depth = velocity.shape[1:]
    steps, parts = surface.shape[:2]
    columns = surface.shape[3]
    n = BELOW + planes + ABOVE
    lanes = steps * CHUNK
    far = pl.BlockSpec(memory_space=pl.ANY)
    scalars = pl.BlockSpec(memory_space=pltpu.SMEM)
    f32 = jnp.float32
    message = pltpu.VMEM((steps, 3, width, depth), f32)
    dma = pltpu.SemaphoreType.DMA
    shapes = (
        jax.ShapeDtypeStruct((1, 3, planes, width, depth), f32),
        jax.ShapeDtypeStruct((1, 6, planes, width, depth), f32),
    )
    vel, sig = pl.pallas_call(
        functools.partial(kernel, groups, slabs, steps),
        out_shape=shapes,
        in_specs=[scalars] * 3 + [far] * 6,
        out_specs=(far, far),
        scratch_shapes=[
            pltpu.VMEM((3, n, width + 8, depth), f32),
            pltpu.VMEM((6, n, width + TOP, depth), f32),
            pltpu.VMEM((3, n, width, depth), f32),
            pltpu.VMEM((3, planes, width, depth), jnp.bfloat16),
            pltpu.VMEM((steps * parts, planes, columns), f32),
            pltpu.VMEM((lanes, 128), f32),
            pltpu.VMEM((columns, lanes), f32),
            pltpu.VMEM((groups, columns, lanes), f32),
            pltpu.VMEM((groups, columns, lanes), f32),
            pltpu.VMEM((groups, columns, lanes), f32),
            pltpu.VMEM((3, width, lanes), f32),
            pltpu.VMEM((steps, 3, width, 128), f32),
            message,
            message,
            message,
            message,
            pltpu.VMEM((3, width, depth), f32),
            pltpu.VMEM((3, planes, width, depth), f32),
            pltpu.VMEM((6, planes, width, depth), f32),
            dma((6,)),
            dma((3, groups)),
            dma((3, groups)),
            dma((6,)),
            dma((6,)),
            dma((steps,)),
            dma((steps,)),
            dma((steps,)),
            dma((steps,)),
            dma((2, planes)),
        ],
        compiler_params=pltpu.CompilerParams(
            collective_id=0, has_side_effects=True, vmem_limit_bytes=VMEM
        ),
    )(
        block_owner,
        candidates.T,
        candidate_of_group,
        velocity,
        stress,
        lame_lambda,
        shear_modulus,
        buoyancy,
        surface.reshape(steps * parts, planes, columns),
    )
    return pl.pallas_call(
        hand_over,
        out_shape=shapes,
        in_specs=[far, far],
        out_specs=(far, far),
        scratch_shapes=[
            pltpu.VMEM((3, planes, width, depth), f32),
            pltpu.VMEM((6, planes, width, depth), f32),
            dma((9,)),
            dma((9,)),
        ],
        compiler_params=pltpu.CompilerParams(vmem_limit_bytes=VMEM),
    )(vel, sig)


def solution(mesh):
    in_specs = (
        P(None, "slab", None, None),
        P(None, "slab", None, None),
        P("slab", None, None),
        P("slab", None, None),
        P("slab", None, None),
        P(None, None, "slab", "cand"),
        P(),
        P(),
        P(),
    )
    out_specs = (P("cand", None, "slab", None, None), P("cand", None, "slab", None, None))
    return jax.shard_map(
        functools.partial(body, mesh.shape["cand"], mesh.shape["slab"]),
        mesh=mesh,
        in_specs=in_specs,
        out_specs=out_specs,
        check_vma=False,
    )
```
